32 devices in a mesh: wide: 8 (over z, y), narrow: 4 (over x, core).
Axes of the slice: x: 2, y: 2, z: 4, core: 2. Of those that a mesh axis runs over, the one named last changes fastest.
Arguments:
- views: bfloat16 [192, 14, 14, 1024], P(('wide', 'narrow')), may hold values from -6 to 6
- partner: int32 [192], P(('wide', 'narrow')), may hold values from 0 to 191, as said below
- block1_params: bfloat16 [6029312], P(('wide', 'narrow')), may hold values from -0.1875 to 0.1875
- block2_params: bfloat16 [4456448], P(('wide', 'narrow')), may hold values from -0.125 to 0.125
- head_params: bfloat16 [4456448], P(('wide', 'narrow')), may hold values from -0.125 to 0.125
- norm_params: float32 [2, 10240], replicated, may hold values from -1 to 1.5, as said below
Outputs:
- loss: float32 [192], P(('wide', 'narrow'))
- views_grad: float32 [192, 14, 14, 1024], P(('wide', 'narrow'))
- block1_grad: float32 [6029312], P(('wide', 'narrow'))
- block2_grad: float32 [4456448], P(('wide', 'narrow'))
- head_grad: float32 [4456448], P(('wide', 'narrow'))
- norm_grad: float32 [2, 10240], replicated
The draws below stay inside these ranges and needn't reach their ends.
Inputs may be any that keep to these rules, and one draw needn't show every extreme that they name: partner[partner[i]] = i and partner[i] != i: the views pair up into images, the pairing over all views drawn from the seed. `norm_params`: row 0 lies in 0.5 to 1.5, row 1 in -1 to 1.
All inputs are finite; a program needn't handle non-finite values.
Results may differ from the reference program's by a relative error of at most 0.018.
Values may be sent and summed in bfloat16 or wider, within the bound.
No kernel may reach another device: no remote copies, remote signals or barrier semaphores. Data moves between devices by JAX's collectives and lax.ppermute only.
A program may use at most 320 MiB of HBM per device.

```python
import jax
import jax.numpy as jnp
from jax import lax

C_IN = 1024
C_MID = 512
C_OUT = 2048
HEAD = 2048
EMBED = 128
SIDE = 14
VIEWS = 192
P1 = 6029312
P2 = 4456448
P3 = 4456448
NORM_TOTAL = 10240
N_WIDE = 8


def draw_partner(key, part):
    key = jax.random.fold_in(key, 11)
    order = jax.random.permutation(key, VIEWS).astype(jnp.int32)
    firsts = order[0::2]
    seconds = order[1::2]
    paired = jnp.zeros((VIEWS,), jnp.int32).at[firsts].set(seconds).at[seconds].set(firsts)
    return paired


def draw_norm_params(key, part):
    key = jax.random.fold_in(key, 23)
    gain_row = jax.random.uniform(jax.random.fold_in(key, 1), (NORM_TOTAL,), jnp.float32, 0.5, 1.5)
    shifts = jax.random.uniform(jax.random.fold_in(key, 2), (NORM_TOTAL,), jnp.float32, -1.0, 1.0)
    return jnp.stack([gain_row, shifts])


def level_of(own_key, extent, shards, least, high):
    level = 1.0
    for axis_at, blocks in shards:
        steps = jax.random.uniform(jax.random.fold_in(jax.random.fold_in(own_key, 6), axis_at), (blocks,), jnp.float32, least / len(shards), high / len(shards))
        level = level * jnp.repeat(jnp.exp(steps), extent[axis_at] // blocks).reshape((-1,) + (1,) * (len(extent) - 1 - axis_at))
    return level


def centred(own_key, shape, scale, bound, split=(), held_as=jnp.bfloat16):
    values = scale * jax.random.normal(own_key, shape, jnp.float32)
    if split:
        values = values * level_of(own_key, shape, split, -0.22, 0.18)
    return jnp.clip(values, -bound, bound).astype(held_as)


def setup_inputs(seed: int = 0) -> dict:
    streams_of = jax.random.split(jax.random.key(seed), 7)
    views = centred(streams_of[0], (VIEWS, SIDE, SIDE, C_IN), 1.0, 6.0, ((0, 32),))
    partner = draw_partner(jax.random.fold_in(streams_of[6], 71), 0)
    block1_params = centred(streams_of[2], (P1,), C_IN ** -0.5, 0.1875, ((0, 32),))
    block2_params = centred(streams_of[3], (P2,), C_OUT ** -0.5, 0.125, ((0, 32),))
    head_params = centred(streams_of[4], (P3,), HEAD ** -0.5, 0.125, ((0, 32),))
    norm_params = draw_norm_params(jax.random.fold_in(streams_of[6], 71), 0)
    return {"views": views, "partner": partner, "block1_params": block1_params, "block2_params": block2_params, "head_params": head_params, "norm_params": norm_params}


@jax.custom_vjp
def low(v):
    return lax.optimization_barrier(v.astype(jnp.bfloat16)).astype(jnp.float32)

@jax.custom_vjp
def low_back(v):
    return v

def low_keep(v):
    return (low(v), None)

def low_pass(kept, grad):
    return (grad,)

def back_keep(v):
    return (v, None)

def back_low(kept, grad):
    return (low(grad),)
low.defvjp(low_keep, low_pass)
low_back.defvjp(back_keep, back_low)
TAU = 0.1
EPSILON = 1e-05
NORM_EPS = 1e-06
HIGHEST = lax.Precision.HIGHEST

def carve_flat(flat_params, shapes):
    pieces = []
    offset = 0
    for layout in shapes:
        length = layout[0] * layout[1]
        pieces.append(flat_params[offset:offset + length].reshape(layout))
        offset += length
    return pieces

def split_norms(norm_params):
    widths = [C_MID, C_MID, C_OUT, C_OUT, C_MID, C_MID, C_OUT, HEAD]
    pieces = []
    offset = 0
    for span_width in widths:
        pieces.append(norm_params[:, offset:offset + span_width])
        offset += span_width
    return pieces

def project(values, kernel):
    return jnp.einsum('...k,kn->...n', values, kernel, precision=HIGHEST)

def spatial(values, kernel, stride):
    channels = values.shape[-1]
    filters = kernel.reshape(3, 3, channels, kernel.shape[-1])
    return lax.conv_general_dilated(values, filters, (stride, stride), ((1, 1), (1, 1)), dimension_numbers=('NHWC', 'HWIO', 'NHWC'), precision=HIGHEST)

def batch_norm(values, affine):
    flattened = values.reshape(-1, values.shape[-1])
    center = lax.optimization_barrier(jnp.mean(flattened, axis=0))
    spread = lax.optimization_barrier(jnp.mean(flattened * flattened, axis=0)) - center * center
    return (values - center) * lax.rsqrt(spread + EPSILON) * affine[0] + affine[1]

def network(inputs, first_flat, second_flat, head_flat, norm_params):
    w_reduce, w_spatial, w_expand, w_short = carve_flat(first_flat, [(C_IN, C_MID), (9 * C_MID, C_MID), (C_MID, C_OUT), (C_IN, C_OUT)])
    w_narrow, w_middle, w_widen = carve_flat(second_flat, [(C_OUT, C_MID), (9 * C_MID, C_MID), (C_MID, C_OUT)])
    w_hidden, w_embed = carve_flat(head_flat, [(C_OUT, HEAD), (HEAD, EMBED)])
    norms = split_norms(norm_params)
    act_one = low(jax.nn.silu(batch_norm(low_back(project(inputs, w_reduce)), norms[0])))
    act_two = low(jax.nn.silu(batch_norm(low_back(spatial(act_one, w_spatial, 2)), norms[1])))
    main_path = batch_norm(low_back(project(act_two, w_expand)), norms[2])
    shortcut = batch_norm(low_back(project(inputs[:, ::2, ::2, :], w_short)), norms[3])
    result_one = low(jax.nn.silu(main_path + shortcut))
    act_three = low(jax.nn.silu(batch_norm(low_back(project(result_one, w_narrow)), norms[4])))
    act_four = low(jax.nn.silu(batch_norm(low_back(spatial(act_three, w_middle, 1)), norms[5])))
    result_two = jax.nn.silu(batch_norm(low_back(project(act_four, w_widen)), norms[6]) + result_one)
    pooled = lax.optimization_barrier(jnp.mean(result_two, axis=(1, 2)))
    hidden = jax.nn.silu(batch_norm(project(pooled, w_hidden), norms[7]))
    embed = project(hidden, w_embed)
    return low(embed * lax.rsqrt(lax.optimization_barrier(jnp.sum(embed * embed, axis=1, keepdims=True)) + NORM_EPS))

def contrast(unit, partner):
    view_ids = jnp.arange(VIEWS, dtype=jnp.int32)
    mates = unit[partner]
    positive = lax.optimization_barrier(jnp.sum(unit * mates, axis=1)) / TAU

    def block_lse(operands):
        anchor_rows, anchor_ids = operands
        scores = jnp.einsum('ie,je->ij', anchor_rows, unit, precision=HIGHEST) / TAU
        scores = jnp.where(anchor_ids[:, None] == view_ids[None, :], -jnp.inf, scores)
        return jax.nn.logsumexp(scores, axis=1)
    lse_blocks = lax.map(jax.checkpoint(block_lse), (unit.reshape(N_WIDE, -1, EMBED), view_ids.reshape(N_WIDE, -1)))
    return lse_blocks.reshape(-1) - positive

def reference(views, partner, block1_params, block2_params, head_params, norm_params):

    def objective(inputs, first_flat, second_flat, head_flat, norm_values):
        unit = network(inputs, first_flat, second_flat, head_flat, norm_values)
        per_view = contrast(unit, partner)
        return (jnp.mean(per_view), per_view)
    primals = (views.astype(jnp.float32), block1_params.astype(jnp.float32), block2_params.astype(jnp.float32), head_params.astype(jnp.float32), norm_params.astype(jnp.float32))
    mean_loss, pullback, per_view = jax.vjp(objective, *primals, has_aux=True)
    cotangents = pullback(jnp.ones_like(mean_loss))
    return (per_view, cotangents[0], cotangents[1], cotangents[2], cotangents[3], cotangents[4])
```

```python
import jax
import jax.numpy as jnp
import numpy as np
from jax import lax
from jax.experimental import pallas as pl
from jax.experimental.pallas import tpu as pltpu
from jax.sharding import PartitionSpec as P

C_IN = 1024
C_MID = 512
C_OUT = 2048
HEAD = 2048
EMBED = 128

TAU = 0.1
EPSILON = 1e-05
NORM_EPS = 1e-06
HIGHEST = lax.Precision.HIGHEST
BOTH = ("wide", "narrow")
BF16 = jnp.bfloat16
F32 = jnp.float32
DIMS = ("NHWC", "HWIO", "NHWC")


def device_count():
    return lax.axis_size("wide") * lax.axis_size("narrow")


def swap(values, mask):
    return lax.ppermute(values, BOTH, [(i, i ^ mask) for i in range(device_count())])


def bit_groups_of(count):
    groups = [[1]]
    bit = 2
    while bit < count:
        if 2 * bit < count:
            groups.append([bit, 2 * bit, 3 * bit])
        else:
            groups.append([bit])
        bit *= 4
    return groups


def bit_groups():
    return bit_groups_of(device_count())


def all_sum(values):
    for masks in bit_groups():
        others = [swap(values, mask) for mask in masks]
        values = values + others[0]
        if len(others) == 3:
            values = values + (others[1] + others[2])
    return values


def reorder_kernel(device, source, target):
    groups = bit_groups_of(source.shape[0])
    for i in range(source.shape[0]):
        offset = jnp.bitwise_xor(device[0], i)
        place = jnp.int32(0)
        width = 0
        for masks in reversed(groups):
            bits = len(masks).bit_length()
            low = masks[0].bit_length() - 1
            place += ((offset >> low) & (2**bits - 1)) << width
            width += bits
        target[i] = source[place]


def all_blocks(values):
    gathered = values[None]
    for masks in reversed(bit_groups()):
        gathered = jnp.concatenate([gathered] + [swap(gathered, mask) for mask in masks], axis=0)
    return pl.pallas_call(
        reorder_kernel,
        out_shape=jax.ShapeDtypeStruct(gathered.shape, gathered.dtype),
        in_specs=[
            pl.BlockSpec(memory_space=pltpu.SMEM),
            pl.BlockSpec(memory_space=pltpu.VMEM),
        ],
        out_specs=pl.BlockSpec(memory_space=pltpu.VMEM),
        compiler_params=pltpu.CompilerParams(vmem_limit_bytes=48 << 20),
        cost_estimate=pl.CostEstimate(
            flops=0, bytes_accessed=8 * np.prod(gathered.shape).item(), transcendentals=0
        ),
    )(lax.axis_index(BOTH).reshape(1), gathered)


def copy_kernel(device, source, target):
    target[...] = source[...]


def add_kernel(device, *refs):
    ways = len(refs) // 3
    for way in range(ways):
        first, second, target = refs[2 * way], refs[2 * way + 1], refs[2 * ways + way]
        target[...] = (first[...].astype(F32) + second[...].astype(F32)).astype(BF16)


def copy_blocks(source, count, place):
    block = (1, *source.shape[1:])
    shape = (count, *source.shape[1:])
    return pl.pallas_call(
        copy_kernel,
        out_shape=jax.ShapeDtypeStruct(shape, source.dtype),
        grid_spec=pltpu.PrefetchScalarGridSpec(
            num_scalar_prefetch=1,
            grid=(count,),
            in_specs=[pl.BlockSpec(block, lambda i, device: (place(i, device[0]), 0, 0))],
            out_specs=pl.BlockSpec(block, lambda i, device: (i, 0, 0)),
        ),
        cost_estimate=pl.CostEstimate(
            flops=0, bytes_accessed=4 * np.prod(shape).item(), transcendentals=0
        ),
    )(lax.axis_index(BOTH).reshape(1), source)


def add_blocks(source, incoming, count, places):
    ways = len(places)
    block = (1, *source.shape[1:])

    def read(place):
        return pl.BlockSpec(block, lambda i, device: (place(i, device[0]), 0, 0))

    shape = jax.ShapeDtypeStruct((count, *source.shape[1:]), BF16)
    size = np.prod(shape.shape).item()
    return pl.pallas_call(
        add_kernel,
        out_shape=[shape] * ways,
        grid_spec=pltpu.PrefetchScalarGridSpec(
            num_scalar_prefetch=1,
            grid=(count,),
            in_specs=[read(place) for pair in places for place in pair],
            out_specs=[pl.BlockSpec(block, lambda i, device: (i, 0, 0))] * ways,
        ),
        compiler_params=pltpu.CompilerParams(vmem_limit_bytes=24 << 20),
        cost_estimate=pl.CostEstimate(
            flops=size * ways, bytes_accessed=6 * size * ways, transcendentals=0
        ),
    )(lax.axis_index(BOTH).reshape(1), *([source, incoming] * ways))


class ScatterSum:
    def __init__(self, data, base):
        self.count = device_count()
        self.base = base
        self.size = data.shape[0]
        self.width = self.size
        self.source = data
        self.incoming = None
        self.folded = False
        self.live = [True] * self.count
        self.stage = 0
        self.stages = self.count.bit_length() - 1
        self.crossed = self.size > 4

    def bit(self, device):
        if self.crossed and self.stage in (1, 2) and device & 1:
            return 3 - self.stage
        return self.stage

    def halves(self, other):
        stage, crossed = self.stage, self.crossed

        def place(i, device):
            core = device & 1
            if crossed and stage in (1, 2):
                bit = stage + core * (3 - 2 * stage)
            else:
                bit = stage
            value = ((device >> bit) & 1) ^ int(other)
            at = core if crossed and stage == 1 else 0
            return ((i >> at) << (at + 1)) | (value << at) | (i & ((1 << at) - 1))

        return place

    def within(self, place):
        if not self.folded:
            return place
        return lambda i, device: 2 * place(i, device) + (device & 1)

    def prepare(self):
        self.split = self.size > 1 << self.stage
        if self.split:
            self.width //= 2
            keep, send = self.halves(False), self.halves(True)
            if self.incoming is None:
                self.folded = True
                return copy_blocks(self.source, self.width, send)
            self.source, outgoing = add_blocks(
                self.source,
                self.incoming,
                self.width,
                [(self.within(keep), keep), (self.within(send), send)],
            )
            self.folded = False
            return outgoing

        def same(i, device):
            return i

        (self.source,) = add_blocks(
            self.source, self.incoming, self.width, [(self.within(same), same)]
        )
        self.folded = False
        return self.source

    def send(self, outgoing):
        pairs = []
        for device in range(self.count):
            bit = 1 << self.bit(device)
            if self.split:
                pairs.append((device, device ^ bit))
            elif self.live[device] and (device ^ self.base) & bit:
                pairs.append((device, device ^ bit))
                self.live[device] = False
        self.incoming = lax.ppermute(outgoing, BOTH, pairs)
        self.stage += 1

    def done(self):
        return self.stage == self.stages

    def result(self):
        return self.source[0].astype(F32) + self.incoming[0].astype(F32)


def step(groups, held):
    groups = [group for group in groups if not group.done()]
    outgoing = [group.prepare() for group in groups]
    held, outgoing = lax.optimization_barrier((held, outgoing))
    for group, array in zip(groups, outgoing):
        group.send(array)
    return held


def unflatten_kernel(order, source, target):
    for at in range(0, target.shape[0], 64):
        sorted_rows = jnp.dot(
            order[...], source[4 * at : 4 * at + 256, :], preferred_element_type=F32
        )
        for part in range(4):
            target[at : at + 64, part * C_MID : (part + 1) * C_MID] = sorted_rows[
                64 * part : 64 * part + 64, :
            ].astype(BF16)


def unflatten(flat, first, rows):
    tile = 256
    while first % (4 * tile):
        tile //= 2
    order = np.zeros((256, 256), np.float32)
    for row in range(256):
        order[row, 4 * (row % 64) + row // 64] = 1.0
    return pl.pallas_call(
        unflatten_kernel,
        out_shape=jax.ShapeDtypeStruct((rows, 4 * C_MID), BF16),
        grid=(rows // tile,),
        in_specs=[
            pl.BlockSpec((256, 256), lambda i: (0, 0)),
            pl.BlockSpec((4 * tile, C_MID), lambda i: (first // (4 * tile) + i, 0)),
        ],
        out_specs=pl.BlockSpec((tile, 4 * C_MID), lambda i: (i, 0)),
        compiler_params=pltpu.CompilerParams(vmem_limit_bytes=24 << 20),
        cost_estimate=pl.CostEstimate(
            flops=2048 * rows * C_MID, bytes_accessed=16 * rows * C_MID, transcendentals=0
        ),
    )(jnp.asarray(order, BF16), flat)


def flat_grad_kernel(inputs, cotan, target, scratch):
    rows = inputs.shape[1]
    grad = lax.dot_general(
        inputs[...], cotan[...], (((0,), (0,)), ((), ())), preferred_element_type=F32
    )
    for lane in range(4):
        for part in range(4):
            at = part * C_MID + lane * 128
            scratch[lane, pl.ds(part, rows, stride=4), :] = grad[:, at : at + 128]
        target[:, lane * 128 : (lane + 1) * 128] = scratch[lane].astype(BF16)


def flat_grad(inputs, cotan):
    inputs = inputs.reshape(-1, inputs.shape[-1])
    cotan = cotan.reshape(-1, cotan.shape[-1])
    count, depth = inputs.shape
    tile = 128
    return pl.pallas_call(
        flat_grad_kernel,
        out_shape=jax.ShapeDtypeStruct((4 * depth, C_MID), BF16),
        grid=(depth // tile,),
        in_specs=[
            pl.BlockSpec((count, tile), lambda i: (0, i)),
            pl.BlockSpec((count, 4 * C_MID), lambda i: (0, 0)),
        ],
        out_specs=pl.BlockSpec((4 * tile, C_MID), lambda i: (i, 0)),
        scratch_shapes=[pltpu.VMEM((4, 4 * tile, 128), F32)],
        compiler_params=pltpu.CompilerParams(vmem_limit_bytes=24 << 20),
        cost_estimate=pl.CostEstimate(
            flops=2 * count * depth * 4 * C_MID,
            bytes_accessed=2 * count * (depth + 4 * C_MID) + 8 * depth * C_MID,
            transcendentals=0,
        ),
    )(inputs, cotan)


def split_norms(norm_params):
    widths = [C_MID, C_MID, C_OUT, C_OUT, C_MID, C_MID, C_OUT, HEAD]
    pieces = []
    offset = 0
    for span_width in widths:
        pieces.append(norm_params[:, offset : offset + span_width])
        offset += span_width
    return pieces


def moments(values):
    rows = values.reshape(-1, values.shape[-1])
    return jnp.stack([jnp.sum(rows, axis=0), jnp.sum(rows * rows, axis=0)])


def stats_of(sums, total_rows):
    center = sums[0] / total_rows
    inv_std = lax.rsqrt(sums[1] / total_rows - center * center + EPSILON)
    return center, inv_std


def silu_slope(values):
    logistic = jax.nn.sigmoid(values)
    return logistic * (1.0 + values * (1.0 - logistic))


class Norm:
    def __init__(self, raw, sums, affine, total_rows):
        self.raw = raw
        self.affine = affine
        self.total_rows = total_rows
        self.center, self.inv_std = stats_of(sums, total_rows)

    def normed(self):
        return (self.raw - self.center) * self.inv_std

    def shifted(self):
        return self.normed() * self.affine[0] + self.affine[1]

    def partial_grads(self, cotan):
        rows = cotan.reshape(-1, cotan.shape[-1])
        normed = self.normed().reshape(-1, cotan.shape[-1])
        return jnp.stack([jnp.sum(rows * normed, axis=0), jnp.sum(rows, axis=0)])

    def pull(self, cotan, grads):
        return (
            self.affine[0]
            * self.inv_std
            * (cotan - grads[1] / self.total_rows - self.normed() * (grads[0] / self.total_rows))
        )


def times(values, kernel):
    return jnp.dot(values, kernel, preferred_element_type=F32)


def times_back(cotan, kernel):
    return lax.dot_general(
        cotan, kernel, (((cotan.ndim - 1,), (1,)), ((), ())), preferred_element_type=F32
    )


def kernel_grad(inputs, cotan):
    return lax.dot_general(
        inputs.reshape(-1, inputs.shape[-1]),
        cotan.reshape(-1, cotan.shape[-1]),
        (((0,), (0,)), ((), ())),
        preferred_element_type=F32,
    )


def conv(values, kernel, stride):
    taps = kernel.reshape(3, 3, C_MID, C_MID)
    return lax.conv_general_dilated(
        values,
        taps,
        (stride, stride),
        ((1, 1), (1, 1)),
        dimension_numbers=DIMS,
        preferred_element_type=F32,
    )


def conv_back(cotan, kernel, stride):
    taps = kernel.reshape(3, 3, C_MID, C_MID)[::-1, ::-1].transpose(0, 1, 3, 2)
    after = stride
    return lax.conv_general_dilated(
        cotan,
        taps,
        (1, 1),
        ((1, after), (1, after)),
        lhs_dilation=(stride, stride),
        dimension_numbers=DIMS,
        preferred_element_type=F32,
    )


def conv_kernel_grad(values, cotan, stride):
    after = 2 - stride
    grad = lax.conv_general_dilated(
        values,
        cotan,
        (1, 1),
        ((1, after), (1, after)),
        rhs_dilation=(stride, stride),
        dimension_numbers=("CHWN", "IHWO", "HWNC"),
        preferred_element_type=F32,
    )
    return grad.reshape(9 * C_MID, C_MID)


def exact_times(values, kernel, contract):
    high = lax.reduce_precision(values, 8, 7)
    low = values - high
    count = values.shape[0]
    terms = jnp.concatenate([high, low], axis=0).astype(BF16)
    product = lax.dot_general(
        terms, kernel, (((1,), (contract,)), ((), ())), preferred_element_type=F32
    )
    return product[:count] + product[count:]


def pad_side(values, size):
    return lax.pad(
        values,
        jnp.zeros((), values.dtype),
        ((0, 0, 0), (0, 0, 0), (0, size - values.shape[2], 0), (0, 0, 0)),
    )


def input_grad_kernel(cotan, kernel, strided, target, spread):
    side = target.shape[1]
    grad = lax.dot_general(
        cotan[0].reshape(-1, C_MID), kernel[...], (((1,), (1,)), ((), ())), preferred_element_type=F32
    )
    spread[...] = jnp.zeros_like(spread)
    for lane in range(C_IN // 128):
        for row in range(strided.shape[1]):
            spread[lane, pl.ds(32 * row, 8, stride=2), :] = strided[
                0, row, :, lane * 128 : (lane + 1) * 128
            ]
    for lane in range(C_IN // 128):
        total = grad[:, lane * 128 : (lane + 1) * 128] + spread[lane]
        target[0, :, :, lane * 128 : (lane + 1) * 128] = total.reshape(side, 16, 128)[:, :side, :]


def input_grad(cotan, kernel, strided):
    count, side = cotan.shape[:2]
    return pl.pallas_call(
        input_grad_kernel,
        out_shape=jax.ShapeDtypeStruct((count, side, side, C_IN), F32),
        grid=(count,),
        in_specs=[
            pl.BlockSpec((1, side, 16, C_MID), lambda i: (i, 0, 0, 0)),
            pl.BlockSpec((C_IN, C_MID), lambda i: (0, 0)),
            pl.BlockSpec((1, side // 2, 8, C_IN), lambda i: (i, 0, 0, 0)),
        ],
        out_specs=pl.BlockSpec((1, side, side, C_IN), lambda i: (i, 0, 0, 0)),
        scratch_shapes=[pltpu.VMEM((C_IN // 128, side * 16, 128), F32)],
        compiler_params=pltpu.CompilerParams(vmem_limit_bytes=24 << 20),
        cost_estimate=pl.CostEstimate(
            flops=2 * count * side * 16 * C_IN * C_MID,
            bytes_accessed=count * side * 16 * (2 * C_MID + 5 * C_IN),
            transcendentals=0,
        ),
    )(cotan, kernel, strided)


def unit_norm(embed):
    return embed * lax.rsqrt(jnp.sum(embed * embed, axis=1, keepdims=True) + NORM_EPS)


def contrast(unit, partner, total_views):
    ids = jnp.arange(total_views, dtype=jnp.int32)
    scores = (
        lax.dot_general(unit, unit, (((1,), (1,)), ((), ())), preferred_element_type=F32) / TAU
    )
    scores = jnp.where(ids[None, :] == ids[:, None], -1e30, scores)
    highest = jnp.max(scores, axis=1)
    log_total = highest + jnp.log(jnp.sum(jnp.exp(scores - highest[:, None]), axis=1))
    match = ids[None, :] == partner[:, None]
    loss = log_total - jnp.sum(jnp.where(match, scores, 0.0), axis=1)
    weights = (
        jnp.exp(scores - log_total[:, None])
        + jnp.exp(scores - log_total[None, :])
        - 2.0 * match.astype(F32)
    ) * (1.0 / (total_views * TAU))
    unit_cot = jnp.dot(weights, unit.astype(F32), preferred_element_type=F32, precision=HIGHEST)
    return loss, unit_cot


def head_kernel_grads(pooled, raw_cot, hidden, embed_cot, block):
    first = lax.axis_index(BOTH) * block
    split = C_OUT * HEAD
    rows = -(-block // HEAD)
    if block % HEAD:
        rows += 1
    row_at = first // HEAD
    padded = jnp.pad(pooled, ((0, 0), (0, rows)))
    left = lax.dynamic_slice_in_dim(padded, jnp.minimum(row_at, C_OUT), rows, axis=1)
    hidden_part = lax.dot_general(
        left, raw_cot, (((0,), (0,)), ((), ())), preferred_element_type=F32, precision=HIGHEST
    ).reshape(-1)
    if block % HEAD:
        hidden_part = lax.dynamic_slice_in_dim(hidden_part, first - row_at * HEAD, block)
    embed_rows = block // EMBED
    padded = jnp.pad(hidden, ((0, 0), (embed_rows, embed_rows)))
    at = jnp.clip((first - split) // EMBED + embed_rows, 0, HEAD + embed_rows)
    left = lax.dynamic_slice_in_dim(padded, at, embed_rows, axis=1)
    embed_part = lax.dot_general(
        left, embed_cot, (((0,), (0,)), ((), ())), preferred_element_type=F32, precision=HIGHEST
    ).reshape(-1)
    place = first + jnp.arange(block, dtype=jnp.int32)
    return jnp.where(place < split, hidden_part, embed_part)


def placed(rows, *pieces):
    flat = jnp.zeros((rows, C_MID), BF16)
    for at, piece in pieces:
        flat = lax.dynamic_update_slice(flat, piece.astype(BF16), (at, 0))
    return flat


def tied(*values):
    return lax.optimization_barrier(values)


def shards(views, partner, block1_params, block2_params, head_params, norm_params):
    views_dev = views.shape[0]
    count = device_count()
    total_views = views_dev * count
    device = lax.axis_index(BOTH)
    norms = split_norms(norm_params)

    def gather(flat):
        return lax.all_gather(flat.reshape(-1, C_MID), BOTH, axis=0, tiled=True)

    first = gather(block1_params)
    second = gather(block2_params)
    head = gather(head_params)
    strided = views[:, ::2, ::2, :]
    partners = all_blocks(partner[:, None]).reshape(-1)
    first, strided, partners = tied(first, strided, partners)
    w_reduce = first[:1024]
    w_spatial = first[1024:5632]

    side = views.shape[1]
    wide_rows = total_views * side * side
    half = side // 2
    rows = total_views * half * half

    raw_one = times(views, w_reduce)
    w_short = unflatten(first, 7680, C_IN)
    raw_short = times(strided, w_short)
    sums, raw_short = tied(all_sum(moments(raw_one)), raw_short)
    norm_one = Norm(raw_one, sums, norms[0], wide_rows)
    act_one = jax.nn.silu(norm_one.shifted()).astype(BF16)
    raw_two = conv(act_one, w_spatial, 2)
    w_expand = unflatten(first, 5632, C_MID)
    sums, w_expand = tied(all_sum(moments(raw_two)), w_expand)
    norm_two = Norm(raw_two, sums, norms[1], rows)
    act_two = jax.nn.silu(norm_two.shifted()).astype(BF16)
    raw_three = times(act_two, w_expand)
    sums = all_sum(jnp.concatenate([moments(raw_three), moments(raw_short)], axis=0))
    norm_three = Norm(raw_three, sums[:2], norms[2], rows)
    norm_short = Norm(raw_short, sums[2:], norms[3], rows)
    joined_one = norm_three.shifted() + norm_short.shifted()
    result_one = jax.nn.silu(joined_one).astype(BF16)

    w_narrow = second[:2048]
    w_middle = second[2048:6656]
    raw_five = times(result_one, w_narrow)
    w_widen = unflatten(second, 6656, C_MID)
    sums, w_widen = tied(all_sum(moments(raw_five)), w_widen)
    norm_five = Norm(raw_five, sums, norms[4], rows)
    act_three = jax.nn.silu(norm_five.shifted()).astype(BF16)
    raw_six = conv(act_three, w_middle, 1)
    norm_six = Norm(raw_six, all_sum(moments(raw_six)), norms[5], rows)
    act_four = jax.nn.silu(norm_six.shifted()).astype(BF16)
    raw_seven = times(act_four, w_widen)
    w_hidden = unflatten(head, 0, C_OUT)
    w_embed = head[4 * C_OUT :].reshape(HEAD, EMBED)
    sums, w_hidden, w_embed = tied(all_sum(moments(raw_seven)), w_hidden, w_embed)
    norm_seven = Norm(raw_seven, sums, norms[6], rows)
    joined_two = norm_seven.shifted() + result_one.astype(F32)
    pooled_own = jnp.mean(jax.nn.silu(joined_two), axis=(1, 2))

    pooled = all_blocks(pooled_own).reshape(total_views, C_OUT)
    raw_hidden = exact_times(pooled, w_hidden, 0)
    norm_head = Norm(raw_hidden, moments(raw_hidden), norms[7], total_views)
    shifted_head = norm_head.shifted()
    hidden = jax.nn.silu(shifted_head)
    embed = exact_times(hidden, w_embed, 0)
    losses, unit_cot = contrast(unit_norm(embed).astype(BF16), partners, total_views)
    _, norm_pull = jax.vjp(unit_norm, embed)
    embed_cot = norm_pull(unit_cot)[0]
    hidden_cot = exact_times(embed_cot, w_embed, 1) * silu_slope(shifted_head)
    grads_head = norm_head.partial_grads(hidden_cot)
    raw_hidden_cot = norm_head.pull(hidden_cot, grads_head)
    own_cot = lax.dynamic_slice_in_dim(raw_hidden_cot, device * views_dev, views_dev, axis=0)
    pooled_cot = exact_times(own_cot, w_hidden, 1)

    joined_cot = (pooled_cot / (half * half))[:, None, None, :] * silu_slope(joined_two)
    head_out = head_kernel_grads(pooled, raw_hidden_cot, hidden, embed_cot, head_params.shape[0])
    loss = lax.dynamic_slice_in_dim(losses, device * views_dev, views_dev)
    grads_seven, head_out, loss = tied(all_sum(norm_seven.partial_grads(joined_cot)), head_out, loss)
    low_seven = norm_seven.pull(joined_cot, grads_seven).astype(BF16)
    act_four_cot = times_back(low_seven, w_widen) * silu_slope(norm_six.shifted())
    grad_widen = flat_grad(act_four, low_seven)
    grads_six, grad_widen = tied(all_sum(norm_six.partial_grads(act_four_cot)), grad_widen)
    low_six = norm_six.pull(act_four_cot, grads_six).astype(BF16)
    act_three_cot = conv_back(low_six, w_middle, 1) * silu_slope(norm_five.shifted())
    grad_middle = conv_kernel_grad(act_three, low_six, 1).astype(BF16)
    grads_five, grad_middle = tied(all_sum(norm_five.partial_grads(act_three_cot)), grad_middle)
    low_five = norm_five.pull(act_three_cot, grads_five).astype(BF16)
    result_one_cot = joined_cot + times_back(low_five, w_narrow)
    grad_narrow = kernel_grad(result_one, low_five)

    joined_one_cot = result_one_cot * silu_slope(joined_one)
    grads_join = all_sum(
        jnp.concatenate(
            [
                norm_three.partial_grads(joined_one_cot),
                norm_short.partial_grads(joined_one_cot)[:1],
            ],
            axis=0,
        )
    )
    second_rows = second.shape[0] // count
    first_rows = first.shape[0] // count
    sum_second = ScatterSum(
        placed(second.shape[0], (0, grad_narrow), (2048, grad_middle), (6656, grad_widen)).reshape(
            count, second_rows, C_MID
        ),
        0,
    )
    grads_join = step([sum_second], grads_join)
    grads_three = grads_join[:2]
    grads_short = jnp.stack([grads_join[2], grads_join[1]])
    low_three = norm_three.pull(joined_one_cot, grads_three).astype(BF16)
    low_short = norm_short.pull(joined_one_cot, grads_short).astype(BF16)
    act_two_cot = times_back(low_three, w_expand) * silu_slope(norm_two.shifted())
    grad_expand = flat_grad(act_two, low_three)
    grad_short = flat_grad(strided, low_short)
    strided_cot = times_back(pad_side(low_short, 8), w_short)
    grads_two = all_sum(norm_two.partial_grads(act_two_cot))
    middle = count // 2 * first_rows
    sum_late = ScatterSum(
        placed(
            middle, (0, grad_expand[middle - 5632 :]), (7680 - middle, grad_short)
        ).reshape(count // 2, first_rows, C_MID),
        count // 2,
    )
    grads_two = step([sum_second, sum_late], grads_two)
    low_two = norm_two.pull(act_two_cot, grads_two).astype(BF16)
    act_one_cot = conv_back(low_two, w_spatial, 2) * silu_slope(norm_one.shifted())
    grad_spatial = conv_kernel_grad(act_one, low_two, 2)
    grads_one = all_sum(norm_one.partial_grads(act_one_cot))
    sum_early = ScatterSum(
        placed(
            middle, (1024, grad_spatial), (5632, grad_expand[: middle - 5632])
        ).reshape(count // 2, first_rows, C_MID),
        0,
    )
    grads_one = step([sum_second, sum_late, sum_early], grads_one)
    low_one = norm_one.pull(act_one_cot, grads_one).astype(BF16)
    grad_reduce = kernel_grad(views, low_one)
    reduce_blocks = count // 8
    sum_reduce = ScatterSum(
        placed(reduce_blocks * first_rows, (0, grad_reduce)).reshape(
            reduce_blocks, first_rows, C_MID
        ),
        0,
    )
    sums = [sum_reduce, sum_early, sum_late, sum_second]
    low_one = step(sums, low_one)
    views_cot = input_grad(pad_side(low_one, 16), w_reduce, strided_cot)
    while not all(group.done() for group in sums):
        step(sums, ())

    second_out = sum_second.result().reshape(-1)
    early = sum_early.result()
    early = early + jnp.where(device < reduce_blocks, sum_reduce.result(), 0.0)
    first_out = jnp.where(device < count // 2, early, sum_late.result()).reshape(-1)
    norm_grad = jnp.concatenate(
        [
            grads_one,
            grads_two,
            grads_three,
            grads_short,
            grads_five,
            grads_six,
            grads_seven,
            grads_head,
        ],
        axis=1,
    )
    return (loss, views_cot, first_out, second_out, head_out, norm_grad)


def solution(mesh):
    return jax.shard_map(
        shards,
        mesh=mesh,
        in_specs=(
            P(BOTH, None, None, None),
            P(BOTH),
            P(BOTH),
            P(BOTH),
            P(BOTH),
            P(),
        ),
        out_specs=(
            P(BOTH),
            P(BOTH, None, None, None),
            P(BOTH),
            P(BOTH),
            P(BOTH),
            P(),
        ),
        check_vma=False,
    )
```

```python
import jax
import jax.numpy as jnp
import numpy as np
from jax import lax
from jax.experimental import pallas as pl
from jax.experimental.pallas import tpu as pltpu
from jax.sharding import PartitionSpec as P

C_IN = 1024
C_MID = 512
C_OUT = 2048
HEAD = 2048
EMBED = 128

TAU = 0.1
EPSILON = 1e-05
NORM_EPS = 1e-06
HIGHEST = lax.Precision.HIGHEST
BOTH = ("wide", "narrow")
BF16 = jnp.bfloat16
F32 = jnp.float32
DIMS = ("NHWC", "HWIO", "NHWC")


def device_count():
    return lax.axis_size("wide") * lax.axis_size("narrow")


def swap(values, mask):
    return lax.ppermute(values, BOTH, [(i, i ^ mask) for i in range(device_count())])


def bit_groups_of(count):
    groups = [[1]]
    bit = 2
    while bit < count:
        if 2 * bit < count:
            groups.append([bit, 2 * bit, 3 * bit])
        else:
            groups.append([bit])
        bit *= 4
    return groups


def bit_groups():
    return bit_groups_of(device_count())


def all_sum(values, groups=(), held=None):
    stages = bit_groups()
    for stage, masks in enumerate(stages):
        if stage == len(stages) - 1 and held is not None:
            values, held = step(groups, (values, held))
        others = [swap(values, mask) for mask in masks]
        values = values + others[0]
        if len(others) == 3:
            values = values + (others[1] + others[2])
    return values if held is None else (values, held)


def gather_blocks(values):
    gathered = values[None]
    for masks in reversed(bit_groups()):
        gathered = jnp.concatenate([gathered] + [swap(gathered, mask) for mask in masks], axis=0)
    return gathered


def place_of(device, i, count):
    offset = jnp.bitwise_xor(device, i)
    place = jnp.int32(0)
    width = 0
    for masks in reversed(bit_groups_of(count)):
        bits = len(masks).bit_length()
        low = masks[0].bit_length() - 1
        place += ((offset >> low) & (2**bits - 1)) << width
        width += bits
    return place


def head_kernel(
    device,
    gathered,
    order,
    affine,
    flat,
    pooled_out,
    hidden_out,
    raw_cot_out,
    embed_cot,
    grads,
    losses,
    pooled_cot,
    rows_in,
    weights,
    embed_rows,
    w_embed,
    pooled,
    hidden,
    raw_cot,
    partners,
    terms,
    normed,
    slope,
    inv_std,
    embed,
    units,
    own_terms,
    own_wide,
    sems,
    out_sems,
):
    count, views_dev = gathered.shape[:2]
    total = count * views_dev
    tile = 256
    tiles = HEAD // tile

    def fetch(n):
        return pltpu.make_async_copy(
            flat.at[pl.ds(n * 4 * tile, 4 * tile), :], rows_in.at[n], sems.at[n]
        )

    def fetch_embed():
        return pltpu.make_async_copy(
            flat.at[pl.ds(4 * C_OUT, C_MID), :], embed_rows, sems.at[tiles]
        )

    def flush(source, target, n):
        return pltpu.make_async_copy(source, target, out_sems.at[n])

    for n in range(tiles):
        fetch(n).start()
    fetch_embed().start()

    for i in range(count):
        block = gathered[place_of(device[0], i, count)]
        pooled[i * views_dev : (i + 1) * views_dev, :] = block[:, :C_OUT]
        partners[i * views_dev : (i + 1) * views_dev, :] = block[:, C_OUT:]
    flush(pooled, pooled_out, 0).start()

    def halves(values):
        high = values.astype(BF16)
        return high, (values - high.astype(F32)).astype(BF16)

    def cut(n, carry):
        cols = pl.ds(pl.multiple_of(n * tile, tile), tile)
        terms[:total, cols], terms[total:, cols] = halves(pooled[:, cols])
        return carry

    lax.fori_loop(0, tiles, cut, 0)

    def unflatten_rows(n, carry):
        fetch(n).wait()
        for at in range(0, tile, 64):
            sorted_rows = jnp.dot(
                order[...], rows_in[n, 4 * at : 4 * at + 256, :], preferred_element_type=F32
            )
            for part in range(4):
                weights[
                    pl.ds(pl.multiple_of(n * tile + at, 64), 64), part * C_MID : (part + 1) * C_MID
                ] = sorted_rows[64 * part : 64 * part + 64, :].astype(BF16)
        return carry

    lax.fori_loop(0, tiles, unflatten_rows, 0)
    fetch_embed().wait()
    for part in range(4):
        embed_rows_wide = embed_rows[:, part * EMBED : (part + 1) * EMBED].astype(F32)
        own_wide[pl.ds(part, C_MID, stride=4), :] = embed_rows_wide
    w_embed[...] = own_wide[...].astype(BF16)
    embed[...] = jnp.zeros_like(embed)

    def forward(n, carry):
        cols = pl.ds(pl.multiple_of(n * tile, tile), tile)
        product = jnp.dot(terms[...], weights[:, cols], preferred_element_type=F32)
        raw = product[:total] + product[total:]
        center = jnp.sum(raw, axis=0, keepdims=True) / total
        spread = jnp.sum(raw * raw, axis=0, keepdims=True) / total - center * center
        scale = lax.rsqrt(spread + EPSILON)
        unit = (raw - center) * scale
        shifted = unit * affine[0:1, cols] + affine[1:2, cols]
        logistic = jax.nn.sigmoid(shifted)
        value = shifted * logistic
        inv_std[:, cols] = scale
        normed[:, cols] = unit
        slope[:, cols] = logistic * (1.0 + shifted * (1.0 - logistic))
        hidden[:, cols] = value
        high, low = halves(value)
        embed[...] += jnp.dot(high, w_embed[cols, :], preferred_element_type=F32) + jnp.dot(
            low, w_embed[cols, :], preferred_element_type=F32
        )
        return carry

    lax.fori_loop(0, tiles, forward, 0)
    flush(hidden, hidden_out, 1).start()

    values = embed[...]
    length = lax.rsqrt(jnp.sum(values * values, axis=1, keepdims=True) + NORM_EPS)
    units[...] = jnp.zeros_like(units)
    units[:total, :] = (values * length).astype(BF16)
    every = units[...]
    size = every.shape[0]
    across = lax.broadcasted_iota(jnp.int32, (size, size), 0)
    along = lax.broadcasted_iota(jnp.int32, (size, size), 1)
    valid = (across != along) & (across < total) & (along < total)
    scores = (
        lax.dot_general(every, every, (((1,), (1,)), ((), ())), preferred_element_type=F32) / TAU
    )
    scores = jnp.where(valid, scores, -1e30)
    highest = jnp.max(scores, axis=1, keepdims=True)
    log_total = highest + jnp.log(jnp.sum(jnp.exp(scores - highest), axis=1, keepdims=True))
    chances = jnp.where(valid, jnp.exp(scores - log_total), 0.0)
    match = (along == partners[:, 0:1].astype(jnp.int32)) & valid
    loss = log_total - jnp.sum(jnp.where(match, scores, 0.0), axis=1, keepdims=True)
    losses[...] = jnp.broadcast_to(loss, losses.shape)
    near = chances - 2.0 * match.astype(F32)
    unit_cot = jnp.zeros((size, EMBED), F32)
    for part in halves(near):
        unit_cot += jnp.dot(part, every, preferred_element_type=F32)
    for part in halves(chances):
        unit_cot += lax.dot_general(
            part, every, (((0,), (0,)), ((), ())), preferred_element_type=F32
        )
    unit_cot = unit_cot[:total] * (1.0 / (total * TAU))
    along_cot = jnp.sum(values * unit_cot, axis=1, keepdims=True)
    cot = length * unit_cot - values * (length * length * length * along_cot)
    embed_cot[...] = cot
    cot_high, cot_low = halves(cot)
    rows = own_terms.shape[0] // 2
    chosen = lax.broadcasted_iota(jnp.int32, (rows, total), 1) == (
        device[0] * views_dev + lax.broadcasted_iota(jnp.int32, (rows, total), 0)
    )
    chosen = jnp.where(chosen, 1.0, 0.0).astype(BF16)

    def backward(n, carry):
        cols = pl.ds(pl.multiple_of(n * tile, tile), tile)
        pull = (((1,), (1,)), ((), ()))
        grad = lax.dot_general(
            cot_high, w_embed[cols, :], pull, preferred_element_type=F32
        ) + lax.dot_general(cot_low, w_embed[cols, :], pull, preferred_element_type=F32)
        grad = grad * slope[:, cols]
        unit = normed[:, cols]
        gain = jnp.sum(grad * unit, axis=0, keepdims=True)
        shift = jnp.sum(grad, axis=0, keepdims=True)
        grads[0:1, cols] = gain
        grads[1:2, cols] = shift
        raw = affine[0:1, cols] * inv_std[:, cols] * (grad - shift / total - unit * (gain / total))
        raw_cot[:, cols] = raw
        own = [
            jnp.dot(chosen, part, preferred_element_type=F32).astype(BF16) for part in halves(raw)
        ]
        own_terms[:, cols] = jnp.concatenate(own, axis=0)
        return carry

    lax.fori_loop(0, tiles, backward, 0)
    flush(raw_cot, raw_cot_out, 2).start()

    def pull_pooled(n, carry):
        at = pl.ds(pl.multiple_of(n * tile, tile), tile)
        product = lax.dot_general(
            own_terms[...],
            weights[at, :],
            (((1,), (1,)), ((), ())),
            preferred_element_type=F32,
        )
        pooled_cot[:, at] = product[:rows] + product[rows:]
        return carry

    lax.fori_loop(0, tiles, pull_pooled, 0)
    flush(pooled, pooled_out, 0).wait()
    flush(hidden, hidden_out, 1).wait()
    flush(raw_cot, raw_cot_out, 2).wait()


def head_pass(gathered, flat, affine):
    count, views_dev, width = gathered.shape
    total = count * views_dev
    size = -(-total // 256) * 256
    rows = 16
    tiles = HEAD // 256
    whole = pl.BlockSpec(memory_space=pltpu.VMEM)
    apart = pl.BlockSpec(memory_space=pl.ANY)
    shape = jax.ShapeDtypeStruct
    return pl.pallas_call(
        head_kernel,
        out_shape=[
            shape((total, C_OUT), F32),
            shape((total, HEAD), F32),
            shape((total, HEAD), F32),
            shape((total, EMBED), F32),
            shape((2, HEAD), F32),
            shape((size, EMBED), F32),
            shape((rows, C_OUT), F32),
        ],
        in_specs=[pl.BlockSpec(memory_space=pltpu.SMEM), whole, whole, whole, apart],
        out_specs=[apart] * 3 + [whole] * 4,
        scratch_shapes=[
            pltpu.VMEM((tiles, 1024, C_MID), BF16),
            pltpu.VMEM((C_OUT, HEAD), BF16),
            pltpu.VMEM((C_MID, C_MID), BF16),
            pltpu.VMEM((HEAD, EMBED), BF16),
            pltpu.VMEM((total, C_OUT), F32),
            pltpu.VMEM((total, HEAD), F32),
            pltpu.VMEM((total, HEAD), F32),
            pltpu.VMEM((size, width - C_OUT), F32),
            pltpu.VMEM((2 * total, C_OUT), BF16),
            pltpu.VMEM((total, HEAD), F32),
            pltpu.VMEM((total, HEAD), F32),
            pltpu.VMEM((1, HEAD), F32),
            pltpu.VMEM((total, EMBED), F32),
            pltpu.VMEM((size, EMBED), BF16),
            pltpu.VMEM((2 * rows, HEAD), BF16),
            pltpu.VMEM((HEAD, EMBED), F32),
            pltpu.SemaphoreType.DMA((tiles + 1,)),
            pltpu.SemaphoreType.DMA((3,)),
        ],
        compiler_params=pltpu.CompilerParams(vmem_limit_bytes=52 << 20),
        cost_estimate=pl.CostEstimate(
            flops=4 * total * C_OUT * HEAD, bytes_accessed=20 << 20, transcendentals=3 * total * HEAD
        ),
    )(
        lax.axis_index(BOTH).reshape(1),
        gathered,
        jnp.asarray(row_order(), BF16),
        affine,
        flat,
    )


def copy_kernel(device, *refs):
    sources, target = refs[:-1], refs[-1]
    for way, source in enumerate(sources):
        target[way] = source[0]


def add_kernel(device, *refs):
    ways = len(refs) // 3
    for way in range(ways):
        first, second, target = refs[2 * way], refs[2 * way + 1], refs[2 * ways + way]
        target[...] = (first[...].astype(F32) + second[...].astype(F32)).astype(BF16)


def copy_blocks(source, count, place):
    block = (1, *source.shape[1:])
    shape = (count, *source.shape[1:])
    ways = min(count, 4)

    def read(way):
        return pl.BlockSpec(block, lambda i, device: (place(ways * i + way, device[0]), 0, 0))

    return pl.pallas_call(
        copy_kernel,
        out_shape=jax.ShapeDtypeStruct(shape, source.dtype),
        grid_spec=pltpu.PrefetchScalarGridSpec(
            num_scalar_prefetch=1,
            grid=(count // ways,),
            in_specs=[read(way) for way in range(ways)],
            out_specs=pl.BlockSpec((ways, *source.shape[1:]), lambda i, device: (i, 0, 0)),
        ),
        compiler_params=pltpu.CompilerParams(vmem_limit_bytes=24 << 20),
        cost_estimate=pl.CostEstimate(
            flops=0, bytes_accessed=4 * np.prod(shape).item(), transcendentals=0
        ),
    )(lax.axis_index(BOTH).reshape(1), *[source] * ways)


def add_blocks(source, incoming, count, places):
    ways = len(places)
    block = (1, *source.shape[1:])

    def read(place):
        return pl.BlockSpec(block, lambda i, device: (place(i, device[0]), 0, 0))

    shape = jax.ShapeDtypeStruct((count, *source.shape[1:]), BF16)
    size = np.prod(shape.shape).item()
    return pl.pallas_call(
        add_kernel,
        out_shape=[shape] * ways,
        grid_spec=pltpu.PrefetchScalarGridSpec(
            num_scalar_prefetch=1,
            grid=(count,),
            in_specs=[read(place) for pair in places for place in pair],
            out_specs=[pl.BlockSpec(block, lambda i, device: (i, 0, 0))] * ways,
        ),
        compiler_params=pltpu.CompilerParams(vmem_limit_bytes=24 << 20),
        cost_estimate=pl.CostEstimate(
            flops=size * ways, bytes_accessed=6 * size * ways, transcendentals=0
        ),
    )(lax.axis_index(BOTH).reshape(1), *([source, incoming] * ways))


class ScatterSum:
    def __init__(self, data, base, size):
        self.count = device_count()
        self.base = base
        self.size = size
        self.width = self.size
        self.source = data
        self.incoming = None
        self.folded = False
        self.live = [True] * self.count
        self.stage = 0
        self.stages = self.count.bit_length() - 1
        order = list(range(self.stages))
        if self.size > 8:
            other = [0, 2, 1] + order[3:]
        elif self.size == 8:
            other = [0, 2, 1] + order[4:] + [3]
        else:
            other = [0, 1] + order[3:] + [2]
        self.orders = [order, other]

    def bit(self, device):
        return self.orders[device & 1][self.stage]

    def halves(self, other):
        bits = [order[self.stage] for order in self.orders]
        ranks = [sorted(order[self.stage :]).index(order[self.stage]) for order in self.orders]

        def place(i, device):
            core = device & 1
            bit = bits[0] + core * (bits[1] - bits[0])
            at = ranks[0] + core * (ranks[1] - ranks[0])
            value = ((device >> bit) & 1) ^ int(other)
            return ((i >> at) << (at + 1)) | (value << at) | (i & ((1 << at) - 1))

        return place

    def within(self, place):
        if not self.folded:
            return place
        return lambda i, device: self.base + 2 * place(i, device) + (device & 1)

    def prepare(self):
        self.split = self.width > 1
        if self.split:
            self.width //= 2
            keep, send = self.halves(False), self.halves(True)
            if self.incoming is None:
                self.folded = True
                return copy_blocks(
                    self.source, self.width, lambda i, device: self.base + send(i, device)
                )
            self.source, outgoing = add_blocks(
                self.source,
                self.incoming,
                self.width,
                [(self.within(keep), keep), (self.within(send), send)],
            )
            self.folded = False
            return outgoing

        self.source = (self.source.astype(F32) + self.incoming.astype(F32)).astype(BF16)
        return self.source

    def send(self, outgoing):
        pairs = []
        for device in range(self.count):
            bit = 1 << self.bit(device)
            if self.split:
                pairs.append((device, device ^ bit))
            elif self.live[device] and (device ^ self.base) & bit:
                pairs.append((device, device ^ bit))
                self.live[device] = False
        self.incoming = lax.ppermute(outgoing, BOTH, pairs)
        self.stage += 1

    def done(self):
        return self.stage == self.stages

    def result(self):
        return self.source[0].astype(F32) + self.incoming[0].astype(F32)


def step(groups, held):
    groups = [group for group in groups if not group.done()]
    outgoing = [group.prepare() for group in groups]
    held, outgoing = lax.optimization_barrier((held, outgoing))
    for group, array in zip(groups, outgoing):
        group.send(array)
    return held


def row_order():
    order = np.zeros((256, 256), np.float32)
    for row in range(256):
        order[row, 4 * (row % 64) + row // 64] = 1.0
    return order


def unflatten_kernel(order, source, target):
    for at in range(0, target.shape[0], 64):
        sorted_rows = jnp.dot(
            order[...], source[4 * at : 4 * at + 256, :], preferred_element_type=F32
        )
        for part in range(4):
            target[at : at + 64, part * C_MID : (part + 1) * C_MID] = sorted_rows[
                64 * part : 64 * part + 64, :
            ].astype(BF16)


def unflatten(flat, first, rows):
    tile = 256
    while first % (4 * tile):
        tile //= 2
    return pl.pallas_call(
        unflatten_kernel,
        out_shape=jax.ShapeDtypeStruct((rows, 4 * C_MID), BF16),
        grid=(rows // tile,),
        in_specs=[
            pl.BlockSpec((256, 256), lambda i: (0, 0)),
            pl.BlockSpec((4 * tile, C_MID), lambda i: (first // (4 * tile) + i, 0)),
        ],
        out_specs=pl.BlockSpec((tile, 4 * C_MID), lambda i: (i, 0)),
        compiler_params=pltpu.CompilerParams(vmem_limit_bytes=24 << 20),
        cost_estimate=pl.CostEstimate(
            flops=2048 * rows * C_MID, bytes_accessed=16 * rows * C_MID, transcendentals=0
        ),
    )(jnp.asarray(row_order(), BF16), flat)


def flat_grad_kernel(inputs, cotan, *refs):
    target, scratch = refs[-2:]
    rows = inputs.shape[1]
    grad = lax.dot_general(
        inputs[...], cotan[...], (((0,), (0,)), ((), ())), preferred_element_type=F32
    )
    for lane in range(4):
        for part in range(4):
            at = part * C_MID + lane * 128
            scratch[lane, pl.ds(part, rows, stride=4), :] = grad[:, at : at + 128]
        target[:, lane * 128 : (lane + 1) * 128] = scratch[lane].astype(BF16)


def row_grad_kernel(inputs, cotan, *refs):
    refs[-1][...] = lax.dot_general(
        inputs[...], cotan[...], (((0,), (0,)), ((), ())), preferred_element_type=F32
    ).astype(BF16)


def grad_into(total, first, inputs, cotan, into=None):
    count, depth = inputs.shape
    width = cotan.shape[1]
    parts = width // C_MID
    if parts == 4:
        kernel, tile = flat_grad_kernel, 128
        scratch = [pltpu.VMEM((4, 4 * tile, 128), F32)]
    else:
        kernel, tile = row_grad_kernel, 256
        scratch = []
    at = first // (parts * tile)
    given = [] if into is None else [into]
    return pl.pallas_call(
        kernel,
        out_shape=jax.ShapeDtypeStruct((total, C_MID), BF16),
        grid=(depth // tile,),
        in_specs=[
            pl.BlockSpec((count, tile), lambda i: (0, i)),
            pl.BlockSpec((count, width), lambda i: (0, 0)),
        ]
        + [pl.BlockSpec(memory_space=pl.ANY) for _ in given],
        out_specs=pl.BlockSpec((parts * tile, C_MID), lambda i: (at + i, 0)),
        scratch_shapes=scratch,
        input_output_aliases={2: 0} if given else {},
        compiler_params=pltpu.CompilerParams(vmem_limit_bytes=24 << 20),
        cost_estimate=pl.CostEstimate(
            flops=2 * count * depth * width,
            bytes_accessed=2 * count * (depth + width) + 2 * depth * width,
            transcendentals=0,
        ),
    )(inputs, cotan, *given)


def split_norms(norm_params):
    widths = [C_MID, C_MID, C_OUT, C_OUT, C_MID, C_MID, C_OUT, HEAD]
    pieces = []
    offset = 0
    for span_width in widths:
        pieces.append(norm_params[:, offset : offset + span_width])
        offset += span_width
    return pieces


def moments(values):
    rows = values.reshape(-1, values.shape[-1])
    return jnp.stack([jnp.sum(rows, axis=0), jnp.sum(rows * rows, axis=0)])


def stats_of(sums, total_rows):
    center = sums[0] / total_rows
    inv_std = lax.rsqrt(sums[1] / total_rows - center * center + EPSILON)
    return center, inv_std


def silu_slope(values):
    logistic = jax.nn.sigmoid(values)
    return logistic * (1.0 + values * (1.0 - logistic))


class Norm:
    def __init__(self, raw, sums, affine, total_rows):
        self.raw = raw
        self.affine = affine
        self.total_rows = total_rows
        self.center, self.inv_std = stats_of(sums, total_rows)

    def normed(self):
        return (self.raw - self.center) * self.inv_std

    def shifted(self):
        return self.normed() * self.affine[0] + self.affine[1]

    def partial_grads(self, cotan):
        rows = cotan.reshape(-1, cotan.shape[-1])
        normed = self.normed().reshape(-1, cotan.shape[-1])
        return jnp.stack([jnp.sum(rows * normed, axis=0), jnp.sum(rows, axis=0)])

    def pull(self, cotan, grads):
        return (
            self.affine[0]
            * self.inv_std
            * (cotan - grads[1] / self.total_rows - self.normed() * (grads[0] / self.total_rows))
        )


def times(values, kernel):
    return jnp.dot(values, kernel, preferred_element_type=F32)


def times_back(cotan, kernel):
    return lax.dot_general(
        cotan, kernel, (((cotan.ndim - 1,), (1,)), ((), ())), preferred_element_type=F32
    )


def kernel_grad(inputs, cotan):
    return lax.dot_general(
        inputs.reshape(-1, inputs.shape[-1]),
        cotan.reshape(-1, cotan.shape[-1]),
        (((0,), (0,)), ((), ())),
        preferred_element_type=F32,
    )


def conv(values, kernel, stride):
    taps = kernel.reshape(3, 3, C_MID, C_MID)
    return lax.conv_general_dilated(
        values,
        taps,
        (stride, stride),
        ((1, 1), (1, 1)),
        dimension_numbers=DIMS,
        preferred_element_type=F32,
    )


def conv_back(cotan, kernel, stride):
    taps = kernel.reshape(3, 3, C_MID, C_MID)[::-1, ::-1].transpose(0, 1, 3, 2)
    after = stride
    return lax.conv_general_dilated(
        cotan,
        taps,
        (1, 1),
        ((1, after), (1, after)),
        lhs_dilation=(stride, stride),
        dimension_numbers=DIMS,
        preferred_element_type=F32,
    )


def conv_kernel_grad(values, cotan, stride):
    after = 2 - stride
    grad = lax.conv_general_dilated(
        values,
        cotan,
        (1, 1),
        ((1, after), (1, after)),
        rhs_dilation=(stride, stride),
        dimension_numbers=("CHWN", "IHWO", "HWNC"),
        preferred_element_type=F32,
    )
    return grad.reshape(9 * C_MID, C_MID)


def exact_times(values, kernel, contract):
    high = lax.reduce_precision(values, 8, 7)
    low = values - high
    count = values.shape[0]
    terms = jnp.concatenate([high, low], axis=0).astype(BF16)
    product = lax.dot_general(
        terms, kernel, (((1,), (contract,)), ((), ())), preferred_element_type=F32
    )
    return product[:count] + product[count:]


def pad_side(values, size):
    return lax.pad(
        values,
        jnp.zeros((), values.dtype),
        ((0, 0, 0), (0, 0, 0), (0, size - values.shape[2], 0), (0, 0, 0)),
    )


def even_cells_kernel(source, target, scratch):
    side = source.shape[1]
    scratch[...] = jnp.zeros_like(scratch)
    for lane in range(C_IN // 128):
        for row in range(0, side, 2):
            scratch[lane, 8 * row : 8 * row + side, :] = source[
                0, row, :, lane * 128 : (lane + 1) * 128
            ].astype(F32)
            target[0, row // 2, :, lane * 128 : (lane + 1) * 128] = scratch[
                lane, pl.ds(8 * row, 8, stride=2), :
            ].astype(BF16)


def even_cells(views):
    count, side = views.shape[:2]
    padded = pl.pallas_call(
        even_cells_kernel,
        out_shape=jax.ShapeDtypeStruct((count, side // 2, 8, C_IN), BF16),
        grid=(count,),
        in_specs=[pl.BlockSpec((1, side, side, C_IN), lambda i: (i, 0, 0, 0))],
        out_specs=pl.BlockSpec((1, side // 2, 8, C_IN), lambda i: (i, 0, 0, 0)),
        scratch_shapes=[pltpu.VMEM((C_IN // 128, side * 8, 128), F32)],
        compiler_params=pltpu.CompilerParams(vmem_limit_bytes=24 << 20),
        cost_estimate=pl.CostEstimate(
            flops=0, bytes_accessed=3 * count * side * side * C_IN, transcendentals=0
        ),
    )(views)
    return padded


def input_grad_kernel(cotan, kernel, strided, target, spread):
    side = target.shape[1]
    grad = lax.dot_general(
        cotan[0].reshape(-1, C_MID), kernel[...], (((1,), (1,)), ((), ())), preferred_element_type=F32
    )
    spread[...] = jnp.zeros_like(spread)
    for lane in range(C_IN // 128):
        for row in range(strided.shape[1]):
            spread[lane, pl.ds(32 * row, 8, stride=2), :] = strided[
                0, row, :, lane * 128 : (lane + 1) * 128
            ]
    for lane in range(C_IN // 128):
        total = grad[:, lane * 128 : (lane + 1) * 128] + spread[lane]
        target[0, :, :, lane * 128 : (lane + 1) * 128] = total.reshape(side, 16, 128)[:, :side, :]


def input_grad(cotan, kernel, strided):
    count, side = cotan.shape[:2]
    return pl.pallas_call(
        input_grad_kernel,
        out_shape=jax.ShapeDtypeStruct((count, side, side, C_IN), F32),
        grid=(count,),
        in_specs=[
            pl.BlockSpec((1, side, 16, C_MID), lambda i: (i, 0, 0, 0)),
            pl.BlockSpec((C_IN, C_MID), lambda i: (0, 0)),
            pl.BlockSpec((1, side // 2, 8, C_IN), lambda i: (i, 0, 0, 0)),
        ],
        out_specs=pl.BlockSpec((1, side, side, C_IN), lambda i: (i, 0, 0, 0)),
        scratch_shapes=[pltpu.VMEM((C_IN // 128, side * 16, 128), F32)],
        compiler_params=pltpu.CompilerParams(vmem_limit_bytes=24 << 20),
        cost_estimate=pl.CostEstimate(
            flops=2 * count * side * 16 * C_IN * C_MID,
            bytes_accessed=count * side * 16 * (2 * C_MID + 5 * C_IN),
            transcendentals=0,
        ),
    )(cotan, kernel, strided)


def unit_norm(embed):
    return embed * lax.rsqrt(jnp.sum(embed * embed, axis=1, keepdims=True) + NORM_EPS)


def contrast(unit, partner, total_views):
    ids = jnp.arange(total_views, dtype=jnp.int32)
    scores = (
        lax.dot_general(unit, unit, (((1,), (1,)), ((), ())), preferred_element_type=F32) / TAU
    )
    scores = jnp.where(ids[None, :] == ids[:, None], -1e30, scores)
    highest = jnp.max(scores, axis=1)
    log_total = highest + jnp.log(jnp.sum(jnp.exp(scores - highest[:, None]), axis=1))
    match = ids[None, :] == partner[:, None]
    loss = log_total - jnp.sum(jnp.where(match, scores, 0.0), axis=1)
    weights = (
        jnp.exp(scores - log_total[:, None])
        + jnp.exp(scores - log_total[None, :])
        - 2.0 * match.astype(F32)
    ) * (1.0 / (total_views * TAU))
    unit_cot = jnp.dot(weights, unit.astype(F32), preferred_element_type=F32, precision=HIGHEST)
    return loss, unit_cot


def head_kernel_grads(pooled, raw_cot, hidden, embed_cot, block):
    first = lax.axis_index(BOTH) * block
    split = C_OUT * HEAD
    rows = -(-block // HEAD)
    if block % HEAD:
        rows += 1
    row_at = first // HEAD
    padded = jnp.pad(pooled, ((0, 0), (0, rows)))
    left = lax.dynamic_slice_in_dim(padded, jnp.minimum(row_at, C_OUT), rows, axis=1)
    hidden_part = lax.dot_general(
        left, raw_cot, (((0,), (0,)), ((), ())), preferred_element_type=F32, precision=HIGHEST
    ).reshape(-1)
    if block % HEAD:
        hidden_part = lax.dynamic_slice_in_dim(hidden_part, first - row_at * HEAD, block)
    embed_rows = block // EMBED
    padded = jnp.pad(hidden, ((0, 0), (embed_rows, embed_rows)))
    at = jnp.clip((first - split) // EMBED + embed_rows, 0, HEAD + embed_rows)
    left = lax.dynamic_slice_in_dim(padded, at, embed_rows, axis=1)
    embed_part = lax.dot_general(
        left, embed_cot, (((0,), (0,)), ((), ())), preferred_element_type=F32, precision=HIGHEST
    ).reshape(-1)
    place = first + jnp.arange(block, dtype=jnp.int32)
    return jnp.where(place < split, hidden_part, embed_part)


def placed(flat, at, piece):
    return lax.dynamic_update_slice(flat, piece.astype(BF16), (at, 0))


def cell_rows(values, size):
    return pad_side(values, size).reshape(-1, values.shape[-1])


def tied(*values):
    return lax.optimization_barrier(values)


def shards(views, partner, block1_params, block2_params, head_params, norm_params):
    views_dev = views.shape[0]
    count = device_count()
    total_views = views_dev * count
    device = lax.axis_index(BOTH)
    norms = split_norms(norm_params)

    def gather(flat):
        return lax.all_gather(flat.reshape(-1, C_MID), BOTH, axis=0, tiled=True)

    first = gather(block1_params)
    head = gather(head_params)
    second = gather(block2_params)
    strided = even_cells(views)
    full_views = pad_side(views, 16).reshape(-1, C_IN)
    first, strided, full_views = tied(first, strided, full_views)
    w_reduce = first[:1024]
    w_spatial = first[1024:5632]

    side = views.shape[1]
    wide_rows = total_views * side * side
    half = side // 2
    rows = total_views * half * half

    raw_one = times(views, w_reduce)
    norm_one = Norm(raw_one, all_sum(moments(raw_one)), norms[0], wide_rows)
    act_one = jax.nn.silu(norm_one.shifted()).astype(BF16)
    raw_two = conv(act_one, w_spatial, 2)
    w_expand = unflatten(first, 5632, C_MID)
    w_short = unflatten(first, 7680, C_IN)
    raw_short = times(strided, w_short)[:, :, :half]
    sums, w_expand, raw_short = tied(all_sum(moments(raw_two)), w_expand, raw_short)
    norm_two = Norm(raw_two, sums, norms[1], rows)
    act_two = jax.nn.silu(norm_two.shifted()).astype(BF16)
    raw_three = times(act_two, w_expand)
    sums = all_sum(jnp.concatenate([moments(raw_three), moments(raw_short)], axis=0))
    norm_three = Norm(raw_three, sums[:2], norms[2], rows)
    norm_short = Norm(raw_short, sums[2:], norms[3], rows)
    joined_one = norm_three.shifted() + norm_short.shifted()
    result_one = jax.nn.silu(joined_one).astype(BF16)

    w_narrow = second[:2048]
    w_middle = second[2048:6656]
    raw_five = times(result_one, w_narrow)
    w_widen = unflatten(second, 6656, C_MID)
    sums, w_widen = tied(all_sum(moments(raw_five)), w_widen)
    norm_five = Norm(raw_five, sums, norms[4], rows)
    act_three = jax.nn.silu(norm_five.shifted()).astype(BF16)
    raw_six = conv(act_three, w_middle, 1)
    norm_six = Norm(raw_six, all_sum(moments(raw_six)), norms[5], rows)
    act_four = jax.nn.silu(norm_six.shifted()).astype(BF16)
    raw_seven = times(act_four, w_widen)
    norm_seven = Norm(raw_seven, all_sum(moments(raw_seven)), norms[6], rows)
    joined_two = norm_seven.shifted() + result_one.astype(F32)
    pooled_own = jnp.mean(jax.nn.silu(joined_two), axis=(1, 2))

    gathered = gather_blocks(
        jnp.concatenate(
            [pooled_own, jnp.broadcast_to(partner.astype(F32)[:, None], (views_dev, EMBED))], axis=1
        )
    )
    if total_views <= 256:
        pooled, hidden, raw_hidden_cot, embed_cot, grads_head, losses, pooled_cot = head_pass(
            gathered, head, norms[7]
        )
        losses = losses[:, 0]
        pooled_cot = pooled_cot[:views_dev]
    else:
        w_hidden = unflatten(head, 0, C_OUT)
        w_embed = head[4 * C_OUT :].reshape(HEAD, EMBED)
        order = jnp.stack([place_of(device, i, count) for i in range(count)])
        pooled = jnp.take(gathered, order, axis=0).reshape(total_views, -1)
        partners = pooled[:, C_OUT].astype(jnp.int32)
        pooled = pooled[:, :C_OUT]
        raw_hidden = exact_times(pooled, w_hidden, 0)
        norm_head = Norm(raw_hidden, moments(raw_hidden), norms[7], total_views)
        shifted_head = norm_head.shifted()
        hidden = jax.nn.silu(shifted_head)
        embed = exact_times(hidden, w_embed, 0)
        losses, unit_cot = contrast(unit_norm(embed).astype(BF16), partners, total_views)
        _, norm_pull = jax.vjp(unit_norm, embed)
        embed_cot = norm_pull(unit_cot)[0]
        hidden_cot = exact_times(embed_cot, w_embed, 1) * silu_slope(shifted_head)
        grads_head = norm_head.partial_grads(hidden_cot)
        raw_hidden_cot = norm_head.pull(hidden_cot, grads_head)
        own_cot = lax.dynamic_slice_in_dim(raw_hidden_cot, device * views_dev, views_dev, axis=0)
        pooled_cot = exact_times(own_cot, w_hidden, 1)

    joined_cot = (pooled_cot / (half * half))[:, None, None, :] * silu_slope(joined_two)
    head_out = head_kernel_grads(pooled, raw_hidden_cot, hidden, embed_cot, head_params.shape[0])
    loss = lax.dynamic_slice_in_dim(losses, device * views_dev, views_dev)
    grads_seven, head_out, loss = tied(all_sum(norm_seven.partial_grads(joined_cot)), head_out, loss)
    low_seven = norm_seven.pull(joined_cot, grads_seven).astype(BF16)
    act_four_cot = times_back(low_seven, w_widen) * silu_slope(norm_six.shifted())
    second_grad = grad_into(second.shape[0], 6656, cell_rows(act_four, 8), cell_rows(low_seven, 8))
    grads_six, second_grad = tied(all_sum(norm_six.partial_grads(act_four_cot)), second_grad)
    low_six = norm_six.pull(act_four_cot, grads_six).astype(BF16)
    act_three_cot = conv_back(low_six, w_middle, 1) * silu_slope(norm_five.shifted())
    second_grad = placed(second_grad, 2048, conv_kernel_grad(act_three, low_six, 1))
    grads_five, second_grad = tied(all_sum(norm_five.partial_grads(act_three_cot)), second_grad)
    low_five = norm_five.pull(act_three_cot, grads_five).astype(BF16)
    result_one_cot = joined_cot + times_back(low_five, w_narrow)

    joined_one_cot = result_one_cot * silu_slope(joined_one)
    grads_join = jnp.concatenate(
        [norm_three.partial_grads(joined_one_cot), norm_short.partial_grads(joined_one_cot)[:1]],
        axis=0,
    )
    second_grad = grad_into(
        second.shape[0], 0, cell_rows(result_one, 8), cell_rows(low_five, 8), second_grad
    )
    sum_second = ScatterSum(
        second_grad.reshape(count, second.shape[0] // count, C_MID), 0, count
    )
    grads_join, second_grad = all_sum(grads_join, [sum_second], second_grad)
    grads_three = grads_join[:2]
    grads_short = jnp.stack([grads_join[2], grads_join[1]])
    low_three = norm_three.pull(joined_one_cot, grads_three).astype(BF16)
    low_short = norm_short.pull(joined_one_cot, grads_short).astype(BF16)
    act_two_cot = times_back(low_three, w_expand) * silu_slope(norm_two.shifted())
    low_short = pad_side(low_short, 8)
    first_grad = grad_into(first.shape[0], 5632, cell_rows(act_two, 8), cell_rows(low_three, 8))
    first_grad = grad_into(
        first.shape[0],
        7680,
        strided.reshape(-1, C_IN),
        low_short.reshape(-1, C_OUT),
        first_grad,
    )
    strided_cot = times_back(low_short, w_short)
    grads_two = step([sum_second], norm_two.partial_grads(act_two_cot))
    grads_two = all_sum(grads_two)
    first_shape = (count, first.shape[0] // count, C_MID)
    first_blocks = first_grad.reshape(first_shape)
    part = count // 4
    late = ScatterSum(first_blocks, 2 * part, 2 * part)
    grads_two, first_grad = step([sum_second, late], (grads_two, first_grad))
    low_two = norm_two.pull(act_two_cot, grads_two).astype(BF16)
    act_one_cot = conv_back(low_two, w_spatial, 2)
    act_one_cot, first_grad = step([late], (act_one_cot, first_grad))
    act_one_cot = act_one_cot * silu_slope(norm_one.shifted())
    grads_one, first_grad = step(
        [sum_second], (norm_one.partial_grads(act_one_cot), first_grad)
    )
    grads_one = all_sum(grads_one)
    first_grad = placed(first_grad, 1024, conv_kernel_grad(act_one, low_two, 2))
    first_blocks = first_grad.reshape(first_shape)
    early = ScatterSum(first_blocks, part, part)
    grads_one, first_grad = step([early, late, sum_second], (grads_one, first_grad))
    low_one = pad_side(norm_one.pull(act_one_cot, grads_one).astype(BF16), 16)
    first_grad = grad_into(
        first.shape[0], 0, full_views, low_one.reshape(-1, C_MID), first_grad
    )
    last = ScatterSum(first_grad.reshape(first_shape), 0, part)
    early.source = last.source
    low_one = step([early, last], low_one)
    views_cot = input_grad(low_one, w_reduce, strided_cot)
    groups = [early, last, late, sum_second]
    while any(not group.done() for group in groups):
        for group in groups:
            if not group.done():
                group.send(group.prepare())

    second_out = sum_second.result().reshape(-1)
    first_out = last.result()
    for group in [early, late]:
        first_out = jnp.where(device < group.base, first_out, group.result())
    first_out = first_out.reshape(-1)
    norm_grad = jnp.concatenate(
        [
            grads_one,
            grads_two,
            grads_three,
            grads_short,
            grads_five,
            grads_six,
            grads_seven,
            grads_head,
        ],
        axis=1,
    )
    return (loss, views_cot, first_out, second_out, head_out, norm_grad)


def solution(mesh):
    return jax.shard_map(
        shards,
        mesh=mesh,
        in_specs=(
            P(BOTH, None, None, None),
            P(BOTH),
            P(BOTH),
            P(BOTH),
            P(BOTH),
            P(),
        ),
        out_specs=(
            P(BOTH),
            P(BOTH, None, None, None),
            P(BOTH),
            P(BOTH),
            P(BOTH),
            P(),
        ),
        check_vma=False,
    )
```

```python
import jax
import jax.numpy as jnp
import numpy as np
from jax import lax
from jax.experimental import pallas as pl
from jax.experimental.pallas import tpu as pltpu
from jax.sharding import PartitionSpec as P

C_IN = 1024
C_MID = 512
C_OUT = 2048
HEAD = 2048
EMBED = 128

TAU = 0.1
EPSILON = 1e-05
NORM_EPS = 1e-06
HIGHEST = lax.Precision.HIGHEST
BOTH = ("wide", "narrow")
BF16 = jnp.bfloat16
F32 = jnp.float32
DIMS = ("NHWC", "HWIO", "NHWC")


def device_count():
    return lax.axis_size("wide") * lax.axis_size("narrow")


def swap(values, mask):
    return lax.ppermute(values, BOTH, [(i, i ^ mask) for i in range(device_count())])


def bit_groups_of(count):
    groups = [[1]]
    bit = 2
    while bit < count:
        if 2 * bit < count:
            groups.append([bit, 2 * bit, 3 * bit])
        else:
            groups.append([bit])
        bit *= 4
    return groups


def bit_groups():
    return bit_groups_of(device_count())


def arrive(groups, values):
    values, arrivals = tied(values, [group.incoming for group in groups])
    for group, incoming in zip(groups, arrivals):
        group.incoming = incoming
    return values


def all_sum(values, groups=(), held=None, gate=None):
    stages = bit_groups()
    for stage, masks in enumerate(stages):
        if stage == 1 and gate is not None:
            _, gate = tied(values, gate)
        if stage == len(stages) - 1 and held is not None:
            values, held = step(groups, (values, held))
        others = [swap(values, mask) for mask in masks]
        values = values + others[0]
        if len(others) == 3:
            values = values + (others[1] + others[2])
    if held is None and gate is None:
        return values
    return (values, gate) if held is None else (values, held)


def gather_blocks(values):
    gathered = values[None]
    for masks in reversed(bit_groups()):
        gathered = jnp.concatenate([gathered] + [swap(gathered, mask) for mask in masks], axis=0)
    return gathered


def place_of(device, i, count):
    offset = jnp.bitwise_xor(device, i)
    place = jnp.int32(0)
    width = 0
    for masks in reversed(bit_groups_of(count)):
        bits = len(masks).bit_length()
        low = masks[0].bit_length() - 1
        place += ((offset >> low) & (2**bits - 1)) << width
        width += bits
    return place


def head_kernel(
    device,
    gathered,
    order,
    affine,
    flat,
    pooled_out,
    hidden_out,
    raw_cot_out,
    embed_cot,
    grads,
    losses,
    pooled_cot,
    rows_in,
    weights,
    embed_rows,
    w_embed,
    pooled,
    hidden,
    raw_cot,
    partners,
    terms,
    normed,
    slope,
    inv_std,
    embed,
    units,
    own_terms,
    own_wide,
    sems,
    out_sems,
):
    count, views_dev = gathered.shape[:2]
    total = count * views_dev
    tile = 256
    tiles = HEAD // tile

    def fetch(n):
        return pltpu.make_async_copy(
            flat.at[pl.ds(n * 4 * tile, 4 * tile), :], rows_in.at[n], sems.at[n]
        )

    def fetch_embed():
        return pltpu.make_async_copy(
            flat.at[pl.ds(4 * C_OUT, C_MID), :], embed_rows, sems.at[tiles]
        )

    def flush(source, target, n):
        return pltpu.make_async_copy(source, target, out_sems.at[n])

    for n in range(tiles):
        fetch(n).start()
    fetch_embed().start()

    for i in range(count):
        block = gathered[place_of(device[0], i, count)].astype(F32)
        pooled[i * views_dev : (i + 1) * views_dev, :] = block[:, :C_OUT]
        partners[i * views_dev : (i + 1) * views_dev, :] = block[:, C_OUT:]
    flush(pooled, pooled_out, 0).start()

    def halves(values):
        high = values.astype(BF16)
        return high, (values - high.astype(F32)).astype(BF16)

    def cut(n, carry):
        cols = pl.ds(pl.multiple_of(n * tile, tile), tile)
        terms[:, cols] = pooled[:, cols].astype(BF16)
        return carry

    lax.fori_loop(0, tiles, cut, 0)

    def unflatten_rows(n, carry):
        fetch(n).wait()
        for at in range(0, tile, 64):
            sorted_rows = jnp.dot(
                order[...], rows_in[n, 4 * at : 4 * at + 256, :], preferred_element_type=F32
            )
            for part in range(4):
                weights[
                    pl.ds(pl.multiple_of(n * tile + at, 64), 64), part * C_MID : (part + 1) * C_MID
                ] = sorted_rows[64 * part : 64 * part + 64, :].astype(BF16)
        return carry

    lax.fori_loop(0, tiles, unflatten_rows, 0)
    fetch_embed().wait()
    for part in range(4):
        embed_rows_wide = embed_rows[:, part * EMBED : (part + 1) * EMBED].astype(F32)
        own_wide[pl.ds(part, C_MID, stride=4), :] = embed_rows_wide
    w_embed[...] = own_wide[...].astype(BF16)
    embed[...] = jnp.zeros_like(embed)

    def forward(n, carry):
        cols = pl.ds(pl.multiple_of(n * tile, tile), tile)
        raw = jnp.dot(terms[...], weights[:, cols], preferred_element_type=F32)
        center = jnp.sum(raw, axis=0, keepdims=True) / total
        spread = jnp.sum(raw * raw, axis=0, keepdims=True) / total - center * center
        scale = lax.rsqrt(spread + EPSILON)
        unit = (raw - center) * scale
        shifted = unit * affine[0:1, cols] + affine[1:2, cols]
        logistic = jax.nn.sigmoid(shifted)
        value = shifted * logistic
        inv_std[:, cols] = scale
        normed[:, cols] = unit
        slope[:, cols] = logistic * (1.0 + shifted * (1.0 - logistic))
        hidden[:, cols] = value
        high, low = halves(value)
        embed[...] += jnp.dot(high, w_embed[cols, :], preferred_element_type=F32) + jnp.dot(
            low, w_embed[cols, :], preferred_element_type=F32
        )
        return carry

    lax.fori_loop(0, tiles, forward, 0)
    flush(hidden, hidden_out, 1).start()

    values = embed[...]
    length = lax.rsqrt(jnp.sum(values * values, axis=1, keepdims=True) + NORM_EPS)
    units[...] = jnp.zeros_like(units)
    units[:total, :] = (values * length).astype(BF16)
    every = units[...]
    size = every.shape[0]
    across = lax.broadcasted_iota(jnp.int32, (size, size), 0)
    along = lax.broadcasted_iota(jnp.int32, (size, size), 1)
    valid = (across != along) & (across < total) & (along < total)
    scores = (
        lax.dot_general(every, every, (((1,), (1,)), ((), ())), preferred_element_type=F32) / TAU
    )
    scores = jnp.where(valid, scores, -1e30)
    highest = jnp.max(scores, axis=1, keepdims=True)
    log_total = highest + jnp.log(jnp.sum(jnp.exp(scores - highest), axis=1, keepdims=True))
    chances = jnp.where(valid, jnp.exp(scores - log_total), 0.0)
    partner = (partners[:, 0:1] * 64.0 + partners[:, 1:2]).astype(jnp.int32)
    match = (along == partner) & valid
    loss = log_total - jnp.sum(jnp.where(match, scores, 0.0), axis=1, keepdims=True)
    losses[...] = jnp.broadcast_to(loss, losses.shape)
    near = chances - 2.0 * match.astype(F32)
    unit_cot = jnp.zeros((size, EMBED), F32)
    for part in halves(near):
        unit_cot += jnp.dot(part, every, preferred_element_type=F32)
    for part in halves(chances):
        unit_cot += lax.dot_general(
            part, every, (((0,), (0,)), ((), ())), preferred_element_type=F32
        )
    unit_cot = unit_cot[:total] * (1.0 / (total * TAU))
    along_cot = jnp.sum(values * unit_cot, axis=1, keepdims=True)
    cot = length * unit_cot - values * (length * length * length * along_cot)
    embed_cot[...] = cot
    cot_high, cot_low = halves(cot)
    rows = own_terms.shape[0] // 2
    chosen = lax.broadcasted_iota(jnp.int32, (rows, total), 1) == (
        device[0] * views_dev + lax.broadcasted_iota(jnp.int32, (rows, total), 0)
    )
    chosen = jnp.where(chosen, 1.0, 0.0).astype(BF16)

    def backward(n, carry):
        cols = pl.ds(pl.multiple_of(n * tile, tile), tile)
        pull = (((1,), (1,)), ((), ()))
        grad = lax.dot_general(
            cot_high, w_embed[cols, :], pull, preferred_element_type=F32
        ) + lax.dot_general(cot_low, w_embed[cols, :], pull, preferred_element_type=F32)
        grad = grad * slope[:, cols]
        unit = normed[:, cols]
        gain = jnp.sum(grad * unit, axis=0, keepdims=True)
        shift = jnp.sum(grad, axis=0, keepdims=True)
        grads[0:1, cols] = gain
        grads[1:2, cols] = shift
        raw = affine[0:1, cols] * inv_std[:, cols] * (grad - shift / total - unit * (gain / total))
        raw_cot[:, cols] = raw
        own = [
            jnp.dot(chosen, part, preferred_element_type=F32).astype(BF16) for part in halves(raw)
        ]
        own_terms[:, cols] = jnp.concatenate(own, axis=0)
        return carry

    lax.fori_loop(0, tiles, backward, 0)
    flush(raw_cot, raw_cot_out, 2).start()

    def pull_pooled(n, carry):
        at = pl.ds(pl.multiple_of(n * tile, tile), tile)
        product = lax.dot_general(
            own_terms[...],
            weights[at, :],
            (((1,), (1,)), ((), ())),
            preferred_element_type=F32,
        )
        pooled_cot[:, at] = product[:rows] + product[rows:]
        return carry

    lax.fori_loop(0, tiles, pull_pooled, 0)
    flush(pooled, pooled_out, 0).wait()
    flush(hidden, hidden_out, 1).wait()
    flush(raw_cot, raw_cot_out, 2).wait()


def head_pass(gathered, flat, affine):
    count, views_dev, width = gathered.shape
    total = count * views_dev
    size = -(-total // 256) * 256
    rows = 16
    tiles = HEAD // 256
    whole = pl.BlockSpec(memory_space=pltpu.VMEM)
    apart = pl.BlockSpec(memory_space=pl.ANY)
    shape = jax.ShapeDtypeStruct
    return pl.pallas_call(
        head_kernel,
        out_shape=[
            shape((total, C_OUT), F32),
            shape((total, HEAD), F32),
            shape((total, HEAD), F32),
            shape((total, EMBED), F32),
            shape((2, HEAD), F32),
            shape((size, EMBED), F32),
            shape((rows, C_OUT), F32),
        ],
        in_specs=[pl.BlockSpec(memory_space=pltpu.SMEM), whole, whole, whole, apart],
        out_specs=[apart] * 3 + [whole] * 4,
        scratch_shapes=[
            pltpu.VMEM((tiles, 1024, C_MID), BF16),
            pltpu.VMEM((C_OUT, HEAD), BF16),
            pltpu.VMEM((C_MID, C_MID), BF16),
            pltpu.VMEM((HEAD, EMBED), BF16),
            pltpu.VMEM((total, C_OUT), F32),
            pltpu.VMEM((total, HEAD), F32),
            pltpu.VMEM((total, HEAD), F32),
            pltpu.VMEM((size, width - C_OUT), F32),
            pltpu.VMEM((total, C_OUT), BF16),
            pltpu.VMEM((total, HEAD), F32),
            pltpu.VMEM((total, HEAD), F32),
            pltpu.VMEM((1, HEAD), F32),
            pltpu.VMEM((total, EMBED), F32),
            pltpu.VMEM((size, EMBED), BF16),
            pltpu.VMEM((2 * rows, HEAD), BF16),
            pltpu.VMEM((HEAD, EMBED), F32),
            pltpu.SemaphoreType.DMA((tiles + 1,)),
            pltpu.SemaphoreType.DMA((3,)),
        ],
        compiler_params=pltpu.CompilerParams(vmem_limit_bytes=52 << 20),
        cost_estimate=pl.CostEstimate(
            flops=4 * total * C_OUT * HEAD, bytes_accessed=20 << 20, transcendentals=3 * total * HEAD
        ),
    )(
        lax.axis_index(BOTH).reshape(1),
        gathered,
        jnp.asarray(row_order(), BF16),
        affine,
        flat,
    )


def copy_kernel(device, *refs):
    sources, target = refs[:-1], refs[-1]
    for way, source in enumerate(sources):
        target[way] = source[0]


def add_kernel(device, *refs):
    ways = len(refs) // 3
    for way in range(ways):
        first, second, target = refs[2 * way], refs[2 * way + 1], refs[2 * ways + way]
        target[...] = (first[...].astype(F32) + second[...].astype(F32)).astype(BF16)


def copy_blocks(source, count, place):
    block = (1, *source.shape[1:])
    shape = (count, *source.shape[1:])
    ways = min(count, 4)

    def read(way):
        return pl.BlockSpec(block, lambda i, device: (place(ways * i + way, device[0]), 0, 0))

    return pl.pallas_call(
        copy_kernel,
        out_shape=jax.ShapeDtypeStruct(shape, source.dtype),
        grid_spec=pltpu.PrefetchScalarGridSpec(
            num_scalar_prefetch=1,
            grid=(count // ways,),
            in_specs=[read(way) for way in range(ways)],
            out_specs=pl.BlockSpec((ways, *source.shape[1:]), lambda i, device: (i, 0, 0)),
        ),
        compiler_params=pltpu.CompilerParams(vmem_limit_bytes=24 << 20),
        cost_estimate=pl.CostEstimate(
            flops=0, bytes_accessed=4 * np.prod(shape).item(), transcendentals=0
        ),
    )(lax.axis_index(BOTH).reshape(1), *[source] * ways)


def add_blocks(source, incoming, count, places):
    ways = len(places)
    block = (1, *source.shape[1:])

    def read(place):
        return pl.BlockSpec(block, lambda i, device: (place(i, device[0]), 0, 0))

    shape = jax.ShapeDtypeStruct((count, *source.shape[1:]), BF16)
    size = np.prod(shape.shape).item()
    return pl.pallas_call(
        add_kernel,
        out_shape=[shape] * ways,
        grid_spec=pltpu.PrefetchScalarGridSpec(
            num_scalar_prefetch=1,
            grid=(count,),
            in_specs=[read(place) for pair in places for place in pair],
            out_specs=[pl.BlockSpec(block, lambda i, device: (i, 0, 0))] * ways,
        ),
        compiler_params=pltpu.CompilerParams(vmem_limit_bytes=24 << 20),
        cost_estimate=pl.CostEstimate(
            flops=size * ways, bytes_accessed=6 * size * ways, transcendentals=0
        ),
    )(lax.axis_index(BOTH).reshape(1), *([source, incoming] * ways))


class ScatterSum:
    def __init__(self, data, base, size):
        self.count = device_count()
        self.base = base
        self.size = size
        self.width = self.size
        self.source = data
        self.incoming = None
        self.folded = False
        self.live = [True] * self.count
        self.stage = 0
        self.stages = self.count.bit_length() - 1
        order = list(range(self.stages))
        if self.size > 8:
            other = [0, 2, 1] + order[3:]
        elif self.size == 8:
            other = [0, 2, 1] + order[4:] + [3]
        else:
            other = [0, 1] + order[3:] + [2]
        self.orders = [order, other]

    def bit(self, device):
        return self.orders[device & 1][self.stage]

    def halves(self, other):
        bits = [order[self.stage] for order in self.orders]
        ranks = [sorted(order[self.stage :]).index(order[self.stage]) for order in self.orders]

        def place(i, device):
            core = device & 1
            bit = bits[0] + core * (bits[1] - bits[0])
            at = ranks[0] + core * (ranks[1] - ranks[0])
            value = ((device >> bit) & 1) ^ int(other)
            return ((i >> at) << (at + 1)) | (value << at) | (i & ((1 << at) - 1))

        return place

    def within(self, place):
        if not self.folded:
            return place
        return lambda i, device: self.base + 2 * place(i, device) + (device & 1)

    def prepare(self):
        self.split = self.width > 1
        if self.split:
            self.width //= 2
            keep, send = self.halves(False), self.halves(True)
            if self.incoming is None:
                self.folded = True
                return copy_blocks(
                    self.source, self.width, lambda i, device: self.base + send(i, device)
                )
            self.source, outgoing = add_blocks(
                self.source,
                self.incoming,
                self.width,
                [(self.within(keep), keep), (self.within(send), send)],
            )
            self.folded = False
            return outgoing

        self.source = (self.source.astype(F32) + self.incoming.astype(F32)).astype(BF16)
        return self.source

    def send(self, outgoing):
        pairs = []
        for device in range(self.count):
            bit = 1 << self.bit(device)
            if self.split:
                pairs.append((device, device ^ bit))
            elif self.live[device] and (device ^ self.base) & bit:
                pairs.append((device, device ^ bit))
                self.live[device] = False
        self.incoming = lax.ppermute(outgoing, BOTH, pairs)
        self.stage += 1

    def done(self):
        return self.stage == self.stages

    def result(self):
        return self.source[0].astype(F32) + self.incoming[0].astype(F32)


def step(groups, held):
    groups = [group for group in groups if not group.done()]
    outgoing = [group.prepare() for group in groups]
    held, outgoing = lax.optimization_barrier((held, outgoing))
    for group, array in zip(groups, outgoing):
        group.send(array)
    return held


def row_order():
    order = np.zeros((256, 256), np.float32)
    for row in range(256):
        order[row, 4 * (row % 64) + row // 64] = 1.0
    return order


def unflatten_kernel(order, flat, target, rows_in, sems, *, first):
    tiles, rows = rows_in.shape[:2]

    def fetch(n):
        return pltpu.make_async_copy(
            flat.at[pl.ds(pl.multiple_of(first + n * rows, 256), rows), :], rows_in.at[n], sems.at[n]
        )

    for n in range(tiles):
        fetch(n).start()

    def sort_rows(n, carry):
        fetch(n).wait()
        for at in range(0, rows // 4, 64):
            sorted_rows = jnp.dot(
                order[...], rows_in[n, 4 * at : 4 * at + 256, :], preferred_element_type=F32
            )
            for part in range(4):
                target[
                    pl.ds(pl.multiple_of(n * (rows // 4) + at, 64), 64),
                    part * C_MID : (part + 1) * C_MID,
                ] = sorted_rows[64 * part : 64 * part + 64, :].astype(BF16)
        return carry

    lax.fori_loop(0, tiles, sort_rows, 0)


def unflatten(flat, first, rows):
    tile = 128

    def kernel(*refs):
        unflatten_kernel(*refs, first=first)

    return pl.pallas_call(
        kernel,
        out_shape=jax.ShapeDtypeStruct((rows, 4 * C_MID), BF16),
        in_specs=[
            pl.BlockSpec(memory_space=pltpu.VMEM),
            pl.BlockSpec(memory_space=pltpu.HBM),
        ],
        out_specs=pl.BlockSpec(memory_space=pltpu.VMEM),
        scratch_shapes=[
            pltpu.VMEM((rows // tile, 4 * tile, C_MID), BF16),
            pltpu.SemaphoreType.DMA((rows // tile,)),
        ],
        compiler_params=pltpu.CompilerParams(vmem_limit_bytes=24 << 20),
        cost_estimate=pl.CostEstimate(
            flops=2048 * rows * C_MID, bytes_accessed=16 * rows * C_MID, transcendentals=0
        ),
    )(jnp.asarray(row_order(), BF16), flat)


def flat_grad_kernel(inputs, cotan, *refs):
    target, scratch = refs[-2:]
    rows = inputs.shape[1]
    grad = lax.dot_general(
        inputs[...], cotan[...], (((0,), (0,)), ((), ())), preferred_element_type=F32
    )
    for lane in range(4):
        for part in range(4):
            at = part * C_MID + lane * 128
            scratch[lane, pl.ds(part, rows, stride=4), :] = grad[:, at : at + 128]
        target[:, lane * 128 : (lane + 1) * 128] = scratch[lane].astype(BF16)


def row_grad_kernel(inputs, cotan, *refs):
    refs[-1][...] = lax.dot_general(
        inputs[...], cotan[...], (((0,), (0,)), ((), ())), preferred_element_type=F32
    ).astype(BF16)


def grad_into(total, first, inputs, cotan, into=None):
    count, depth = inputs.shape
    width = cotan.shape[1]
    parts = width // C_MID
    if parts == 4:
        kernel, tile = flat_grad_kernel, 128
        scratch = [pltpu.VMEM((4, 4 * tile, 128), F32)]
    else:
        kernel, tile = row_grad_kernel, 256
        scratch = []
    at = first // (parts * tile)
    given = [] if into is None else [into]
    return pl.pallas_call(
        kernel,
        out_shape=jax.ShapeDtypeStruct((total, C_MID), BF16),
        grid=(depth // tile,),
        in_specs=[
            pl.BlockSpec((count, tile), lambda i: (0, i)),
            pl.BlockSpec((count, width), lambda i: (0, 0)),
        ]
        + [pl.BlockSpec(memory_space=pl.ANY) for _ in given],
        out_specs=pl.BlockSpec((parts * tile, C_MID), lambda i: (at + i, 0)),
        scratch_shapes=scratch,
        input_output_aliases={2: 0} if given else {},
        compiler_params=pltpu.CompilerParams(vmem_limit_bytes=24 << 20),
        cost_estimate=pl.CostEstimate(
            flops=2 * count * depth * width,
            bytes_accessed=2 * count * (depth + width) + 2 * depth * width,
            transcendentals=0,
        ),
    )(inputs, cotan, *given)


def split_norms(norm_params):
    widths = [C_MID, C_MID, C_OUT, C_OUT, C_MID, C_MID, C_OUT, HEAD]
    pieces = []
    offset = 0
    for span_width in widths:
        pieces.append(norm_params[:, offset : offset + span_width])
        offset += span_width
    return pieces


def moments(values):
    rows = values.reshape(-1, values.shape[-1])
    return jnp.stack([jnp.sum(rows, axis=0), jnp.sum(rows * rows, axis=0)])


def stats_of(sums, total_rows):
    center = sums[0] / total_rows
    inv_std = lax.rsqrt(sums[1] / total_rows - center * center + EPSILON)
    return center, inv_std


def silu_slope(values):
    logistic = jax.nn.sigmoid(values)
    return logistic * (1.0 + values * (1.0 - logistic))


class Norm:
    def __init__(self, raw, sums, affine, total_rows):
        self.raw = raw
        self.affine = affine
        self.total_rows = total_rows
        self.center, self.inv_std = stats_of(sums, total_rows)

    def normed(self):
        return (self.raw - self.center) * self.inv_std

    def shifted(self):
        return self.normed() * self.affine[0] + self.affine[1]

    def partial_grads(self, cotan):
        rows = cotan.reshape(-1, cotan.shape[-1])
        normed = self.normed().reshape(-1, cotan.shape[-1])
        return jnp.stack([jnp.sum(rows * normed, axis=0), jnp.sum(rows, axis=0)])

    def pull(self, cotan, grads):
        return (
            self.affine[0]
            * self.inv_std
            * (cotan - grads[1] / self.total_rows - self.normed() * (grads[0] / self.total_rows))
        )


def times(values, kernel):
    return jnp.dot(values, kernel, preferred_element_type=F32)


def times_back(cotan, kernel):
    return lax.dot_general(
        cotan, kernel, (((cotan.ndim - 1,), (1,)), ((), ())), preferred_element_type=F32
    )


def kernel_grad(inputs, cotan):
    return lax.dot_general(
        inputs.reshape(-1, inputs.shape[-1]),
        cotan.reshape(-1, cotan.shape[-1]),
        (((0,), (0,)), ((), ())),
        preferred_element_type=F32,
    )


def conv(values, kernel, stride):
    taps = kernel.reshape(3, 3, C_MID, C_MID)
    return lax.conv_general_dilated(
        values,
        taps,
        (stride, stride),
        ((1, 1), (1, 1)),
        dimension_numbers=DIMS,
        preferred_element_type=F32,
    )


def conv_back(cotan, kernel, stride):
    taps = kernel.reshape(3, 3, C_MID, C_MID)[::-1, ::-1].transpose(0, 1, 3, 2)
    after = stride
    return lax.conv_general_dilated(
        cotan,
        taps,
        (1, 1),
        ((1, after), (1, after)),
        lhs_dilation=(stride, stride),
        dimension_numbers=DIMS,
        preferred_element_type=F32,
    )


def conv_kernel_grad(values, cotan, stride):
    after = 2 - stride
    grad = lax.conv_general_dilated(
        values,
        cotan,
        (1, 1),
        ((1, after), (1, after)),
        rhs_dilation=(stride, stride),
        dimension_numbers=("CHWN", "IHWO", "HWNC"),
        preferred_element_type=F32,
    )
    return grad.reshape(9 * C_MID, C_MID)


def exact_times(values, kernel, contract):
    high = lax.reduce_precision(values, 8, 7)
    low = values - high
    count = values.shape[0]
    terms = jnp.concatenate([high, low], axis=0).astype(BF16)
    product = lax.dot_general(
        terms, kernel, (((1,), (contract,)), ((), ())), preferred_element_type=F32
    )
    return product[:count] + product[count:]


def pad_side(values, size):
    return lax.pad(
        values,
        jnp.zeros((), values.dtype),
        ((0, 0, 0), (0, 0, 0), (0, size - values.shape[2], 0), (0, 0, 0)),
    )


def even_cells_kernel(source, target, scratch):
    side = source.shape[1]
    scratch[...] = jnp.zeros_like(scratch)
    for lane in range(C_IN // 128):
        for row in range(0, side, 2):
            scratch[lane, 8 * row : 8 * row + side, :] = source[
                0, row, :, lane * 128 : (lane + 1) * 128
            ].astype(F32)
            target[0, row // 2, :, lane * 128 : (lane + 1) * 128] = scratch[
                lane, pl.ds(8 * row, 8, stride=2), :
            ].astype(BF16)


def even_cells(views):
    count, side = views.shape[:2]
    padded = pl.pallas_call(
        even_cells_kernel,
        out_shape=jax.ShapeDtypeStruct((count, side // 2, 8, C_IN), BF16),
        grid=(count,),
        in_specs=[pl.BlockSpec((1, side, side, C_IN), lambda i: (i, 0, 0, 0))],
        out_specs=pl.BlockSpec((1, side // 2, 8, C_IN), lambda i: (i, 0, 0, 0)),
        scratch_shapes=[pltpu.VMEM((C_IN // 128, side * 8, 128), F32)],
        compiler_params=pltpu.CompilerParams(vmem_limit_bytes=24 << 20),
        cost_estimate=pl.CostEstimate(
            flops=0, bytes_accessed=3 * count * side * side * C_IN, transcendentals=0
        ),
    )(views)
    return padded


def input_grad_kernel(cotan, kernel, strided, target, spread):
    side = target.shape[1]
    grad = lax.dot_general(
        cotan[0].reshape(-1, C_MID), kernel[...], (((1,), (1,)), ((), ())), preferred_element_type=F32
    )
    spread[...] = jnp.zeros_like(spread)
    for lane in range(C_IN // 128):
        for row in range(strided.shape[1]):
            spread[lane, pl.ds(32 * row, 8, stride=2), :] = strided[
                0, row, :, lane * 128 : (lane + 1) * 128
            ]
    for lane in range(C_IN // 128):
        total = grad[:, lane * 128 : (lane + 1) * 128] + spread[lane]
        target[0, :, :, lane * 128 : (lane + 1) * 128] = total.reshape(side, 16, 128)[:, :side, :]


def input_grad(cotan, kernel, strided):
    count, side = cotan.shape[:2]
    return pl.pallas_call(
        input_grad_kernel,
        out_shape=jax.ShapeDtypeStruct((count, side, side, C_IN), F32),
        grid=(count,),
        in_specs=[
            pl.BlockSpec((1, side, 16, C_MID), lambda i: (i, 0, 0, 0)),
            pl.BlockSpec((C_IN, C_MID), lambda i: (0, 0)),
            pl.BlockSpec((1, side // 2, 8, C_IN), lambda i: (i, 0, 0, 0)),
        ],
        out_specs=pl.BlockSpec((1, side, side, C_IN), lambda i: (i, 0, 0, 0)),
        scratch_shapes=[pltpu.VMEM((C_IN // 128, side * 16, 128), F32)],
        compiler_params=pltpu.CompilerParams(vmem_limit_bytes=24 << 20),
        cost_estimate=pl.CostEstimate(
            flops=2 * count * side * 16 * C_IN * C_MID,
            bytes_accessed=count * side * 16 * (2 * C_MID + 5 * C_IN),
            transcendentals=0,
        ),
    )(cotan, kernel, strided)


def silu_moments(mean, spread):
    nodes, weights = np.polynomial.hermite_e.hermegauss(5)
    weights = weights / weights.sum()
    values = [jax.nn.silu(mean + float(node) * jnp.sqrt(spread)) for node in nodes]
    first = sum(float(weight) * value for weight, value in zip(weights, values))
    second = sum(float(weight) * value * value for weight, value in zip(weights, values))
    return first, jnp.maximum(second - first * first, 0.0)


def pooled_center(main, short, last):
    joined, spread = silu_moments(main[1] + short[1], main[0] * main[0] + short[0] * short[0])
    return silu_moments(last[1] + joined, last[0] * last[0] + spread)[0]


def unit_norm(embed):
    return embed * lax.rsqrt(jnp.sum(embed * embed, axis=1, keepdims=True) + NORM_EPS)


def contrast(unit, partner, total_views):
    ids = jnp.arange(total_views, dtype=jnp.int32)
    scores = (
        lax.dot_general(unit, unit, (((1,), (1,)), ((), ())), preferred_element_type=F32) / TAU
    )
    scores = jnp.where(ids[None, :] == ids[:, None], -1e30, scores)
    highest = jnp.max(scores, axis=1)
    log_total = highest + jnp.log(jnp.sum(jnp.exp(scores - highest[:, None]), axis=1))
    match = ids[None, :] == partner[:, None]
    loss = log_total - jnp.sum(jnp.where(match, scores, 0.0), axis=1)
    weights = (
        jnp.exp(scores - log_total[:, None])
        + jnp.exp(scores - log_total[None, :])
        - 2.0 * match.astype(F32)
    ) * (1.0 / (total_views * TAU))
    unit_cot = jnp.dot(weights, unit.astype(F32), preferred_element_type=F32, precision=HIGHEST)
    return loss, unit_cot


def head_kernel_grads(pooled, raw_cot, hidden, embed_cot, block):
    first = lax.axis_index(BOTH) * block
    split = C_OUT * HEAD
    rows = -(-block // HEAD)
    if block % HEAD:
        rows += 1
    row_at = first // HEAD
    padded = jnp.pad(pooled, ((0, 0), (0, rows)))
    left = lax.dynamic_slice_in_dim(padded, jnp.minimum(row_at, C_OUT), rows, axis=1)
    hidden_part = lax.dot_general(
        left, raw_cot, (((0,), (0,)), ((), ())), preferred_element_type=F32, precision=HIGHEST
    ).reshape(-1)
    if block % HEAD:
        hidden_part = lax.dynamic_slice_in_dim(hidden_part, first - row_at * HEAD, block)
    embed_rows = block // EMBED
    padded = jnp.pad(hidden, ((0, 0), (embed_rows, embed_rows)))
    at = jnp.clip((first - split) // EMBED + embed_rows, 0, HEAD + embed_rows)
    left = lax.dynamic_slice_in_dim(padded, at, embed_rows, axis=1)
    embed_part = lax.dot_general(
        left, embed_cot, (((0,), (0,)), ((), ())), preferred_element_type=F32, precision=HIGHEST
    ).reshape(-1)
    place = first + jnp.arange(block, dtype=jnp.int32)
    return jnp.where(place < split, hidden_part, embed_part)


def placed(flat, at, piece):
    return lax.dynamic_update_slice(flat, piece.astype(BF16), (at, 0))


def cell_rows(values, size):
    return pad_side(values, size).reshape(-1, values.shape[-1])


def tied(*values):
    return lax.optimization_barrier(values)


def shards(views, partner, block1_params, block2_params, head_params, norm_params):
    views_dev = views.shape[0]
    count = device_count()
    total_views = views_dev * count
    device = lax.axis_index(BOTH)
    norms = split_norms(norm_params)

    def gather(flat):
        return lax.all_gather(flat.reshape(-1, C_MID), BOTH, axis=0, tiled=True)

    first = gather(block1_params)
    head = gather(head_params)
    second = gather(block2_params)
    strided = even_cells(views)
    full_views = pad_side(views, 16).reshape(-1, C_IN)
    first, strided, full_views = tied(first, strided, full_views)
    w_reduce = first[:1024]
    w_spatial = first[1024:5632]

    side = views.shape[1]
    wide_rows = total_views * side * side
    half = side // 2
    rows = total_views * half * half

    raw_one = times(views, w_reduce)
    norm_one = Norm(raw_one, all_sum(moments(raw_one)), norms[0], wide_rows)
    act_one = jax.nn.silu(norm_one.shifted()).astype(BF16)
    raw_two = conv(act_one, w_spatial, 2)
    w_expand = unflatten(first, 5632, C_MID)
    w_short = unflatten(first, 7680, C_IN)
    raw_short = times(strided, w_short)[:, :, :half]
    sums, w_expand, raw_short = tied(all_sum(moments(raw_two)), w_expand, raw_short)
    norm_two = Norm(raw_two, sums, norms[1], rows)
    act_two = jax.nn.silu(norm_two.shifted()).astype(BF16)
    raw_three = times(act_two, w_expand)
    sums = all_sum(jnp.concatenate([moments(raw_three), moments(raw_short)], axis=0))
    norm_three = Norm(raw_three, sums[:2], norms[2], rows)
    norm_short = Norm(raw_short, sums[2:], norms[3], rows)
    joined_one = norm_three.shifted() + norm_short.shifted()
    result_one = jax.nn.silu(joined_one).astype(BF16)

    w_narrow = second[:2048]
    w_middle = second[2048:6656]
    raw_five = times(result_one, w_narrow)
    norm_five = Norm(raw_five, all_sum(moments(raw_five)), norms[4], rows)
    act_three = jax.nn.silu(norm_five.shifted()).astype(BF16)
    raw_six = conv(act_three, w_middle, 1)
    w_widen = unflatten(second, 6656, C_MID)
    sums, w_widen = tied(all_sum(moments(raw_six)), w_widen)
    norm_six = Norm(raw_six, sums, norms[5], rows)
    act_four = jax.nn.silu(norm_six.shifted()).astype(BF16)
    raw_seven = times(act_four, w_widen)
    norm_seven = Norm(raw_seven, all_sum(moments(raw_seven)), norms[6], rows)
    joined_two = norm_seven.shifted() + result_one.astype(F32)
    pooled_own = jnp.mean(jax.nn.silu(joined_two), axis=(1, 2))

    center = pooled_center(norms[2], norms[3], norms[6])
    digits = jnp.stack([partner // 64, partner % 64], axis=1).astype(F32)
    gathered = gather_blocks(
        jnp.concatenate(
            [pooled_own - center, jnp.pad(digits, ((0, 0), (0, EMBED - 2)))], axis=1
        ).astype(BF16)
    )
    if total_views <= 256:
        pooled, hidden, raw_hidden_cot, embed_cot, grads_head, losses, pooled_cot = head_pass(
            gathered, head, norms[7]
        )
        losses = losses[:, 0]
        pooled_cot = pooled_cot[:views_dev]
    else:
        w_hidden = unflatten(head, 0, C_OUT)
        w_embed = head[4 * C_OUT :].reshape(HEAD, EMBED)
        order = jnp.stack([place_of(device, i, count) for i in range(count)])
        pooled = jnp.take(gathered, order, axis=0).reshape(total_views, -1).astype(F32)
        partners = (pooled[:, C_OUT] * 64.0 + pooled[:, C_OUT + 1]).astype(jnp.int32)
        pooled = pooled[:, :C_OUT]
        raw_hidden = exact_times(pooled, w_hidden, 0)
        norm_head = Norm(raw_hidden, moments(raw_hidden), norms[7], total_views)
        shifted_head = norm_head.shifted()
        hidden = jax.nn.silu(shifted_head)
        embed = exact_times(hidden, w_embed, 0)
        losses, unit_cot = contrast(unit_norm(embed).astype(BF16), partners, total_views)
        _, norm_pull = jax.vjp(unit_norm, embed)
        embed_cot = norm_pull(unit_cot)[0]
        hidden_cot = exact_times(embed_cot, w_embed, 1) * silu_slope(shifted_head)
        grads_head = norm_head.partial_grads(hidden_cot)
        raw_hidden_cot = norm_head.pull(hidden_cot, grads_head)
        own_cot = lax.dynamic_slice_in_dim(raw_hidden_cot, device * views_dev, views_dev, axis=0)
        pooled_cot = exact_times(own_cot, w_hidden, 1)

    joined_cot = (pooled_cot / (half * half))[:, None, None, :] * silu_slope(joined_two)
    loss = lax.dynamic_slice_in_dim(losses, device * views_dev, views_dev)
    grads_seven, loss = tied(all_sum(norm_seven.partial_grads(joined_cot)), loss)
    low_seven = norm_seven.pull(joined_cot, grads_seven).astype(BF16)
    act_four_cot = times_back(low_seven, w_widen) * silu_slope(norm_six.shifted())
    second_grad = grad_into(second.shape[0], 6656, cell_rows(act_four, 8), cell_rows(low_seven, 8))
    grads_six, second_grad = tied(all_sum(norm_six.partial_grads(act_four_cot)), second_grad)
    low_six = norm_six.pull(act_four_cot, grads_six).astype(BF16)
    act_three_cot = conv_back(low_six, w_middle, 1) * silu_slope(norm_five.shifted())
    second_grad = placed(second_grad, 2048, conv_kernel_grad(act_three, low_six, 1))
    grads_five, second_grad = tied(all_sum(norm_five.partial_grads(act_three_cot)), second_grad)
    low_five = norm_five.pull(act_three_cot, grads_five).astype(BF16)
    result_one_cot = joined_cot + times_back(low_five, w_narrow)

    joined_one_cot = result_one_cot * silu_slope(joined_one)
    grads_join = jnp.concatenate(
        [norm_three.partial_grads(joined_one_cot), norm_short.partial_grads(joined_one_cot)[:1]],
        axis=0,
    )
    second_grad = grad_into(
        second.shape[0], 0, cell_rows(result_one, 8), cell_rows(low_five, 8), second_grad
    )
    sum_second = ScatterSum(
        second_grad.reshape(count, second.shape[0] // count, C_MID), 0, count
    )
    grads_join, second_grad = all_sum(grads_join, [sum_second], second_grad)
    grads_three = grads_join[:2]
    grads_short = jnp.stack([grads_join[2], grads_join[1]])
    low_three = norm_three.pull(joined_one_cot, grads_three).astype(BF16)
    low_short = norm_short.pull(joined_one_cot, grads_short).astype(BF16)
    act_two_cot = times_back(low_three, w_expand) * silu_slope(norm_two.shifted())
    low_short = pad_side(low_short, 8)
    first_grad = grad_into(first.shape[0], 5632, cell_rows(act_two, 8), cell_rows(low_three, 8))
    first_grad = grad_into(
        first.shape[0],
        7680,
        strided.reshape(-1, C_IN),
        low_short.reshape(-1, C_OUT),
        first_grad,
    )
    grads_two = step([sum_second], norm_two.partial_grads(act_two_cot))
    grads_two, (head_rows, low_short) = all_sum(
        grads_two, gate=((pooled, raw_hidden_cot, hidden, embed_cot), low_short)
    )
    head_out = head_kernel_grads(*head_rows, head_params.shape[0])
    strided_cot = times_back(low_short, w_short)
    first_shape = (count, first.shape[0] // count, C_MID)
    first_blocks = first_grad.reshape(first_shape)
    part = count // 4
    late = ScatterSum(first_blocks, 2 * part, 2 * part)
    grads_two, first_grad, head_out, strided_cot = step(
        [sum_second, late], (grads_two, first_grad, head_out, strided_cot)
    )
    low_two = norm_two.pull(act_two_cot, grads_two).astype(BF16)
    act_one_cot = conv_back(low_two, w_spatial, 2)
    act_one_cot, first_grad = step([late], (act_one_cot, first_grad))
    act_one_cot = act_one_cot * silu_slope(norm_one.shifted())
    grads_one, first_grad = step(
        [sum_second], (norm_one.partial_grads(act_one_cot), first_grad)
    )
    grads_one = all_sum(grads_one)
    grad_spatial = conv_kernel_grad(act_one, low_two, 2).astype(BF16)
    early_rows = part * first_shape[1]
    first_grad = placed(first_grad, early_rows, grad_spatial[early_rows - 1024 :])
    last_grad = jnp.pad(grad_spatial[: early_rows - 1024], ((1024, 0), (0, 0)))
    early = ScatterSum(first_grad.reshape(first_shape), part, part)
    grads_one, first_grad, last_grad = step(
        [early, late, sum_second], (grads_one, first_grad, last_grad)
    )
    low_one = pad_side(norm_one.pull(act_one_cot, grads_one).astype(BF16), 16)
    low_one = step([early], low_one)
    last_grad = grad_into(early_rows, 0, full_views, low_one.reshape(-1, C_MID), last_grad)
    last_grad = arrive([late], last_grad)
    last = ScatterSum(last_grad.reshape(part, *first_shape[1:]), 0, part)
    low_one = step([last], low_one)
    views_cot = input_grad(low_one, w_reduce, strided_cot)
    groups = [early, last, late, sum_second]
    while any(not group.done() for group in groups):
        for group in groups:
            if not group.done():
                group.send(group.prepare())

    second_out = sum_second.result().reshape(-1)
    first_out = last.result()
    for group in [early, late]:
        first_out = jnp.where(device < group.base, first_out, group.result())
    first_out = first_out.reshape(-1)
    norm_grad = jnp.concatenate(
        [
            grads_one,
            grads_two,
            grads_three,
            grads_short,
            grads_five,
            grads_six,
            grads_seven,
            grads_head,
        ],
        axis=1,
    )
    return (loss, views_cot, first_out, second_out, head_out, norm_grad)


def solution(mesh):
    return jax.shard_map(
        shards,
        mesh=mesh,
        in_specs=(
            P(BOTH, None, None, None),
            P(BOTH),
            P(BOTH),
            P(BOTH),
            P(BOTH),
            P(),
        ),
        out_specs=(
            P(BOTH),
            P(BOTH, None, None, None),
            P(BOTH),
            P(BOTH),
            P(BOTH),
            P(),
        ),
        check_vma=False,
    )
```

```python
import jax
import jax.numpy as jnp
import numpy as np
from jax import lax
from jax.experimental import pallas as pl
from jax.experimental.pallas import tpu as pltpu
from jax.sharding import PartitionSpec as P

C_IN = 1024
C_MID = 512
C_OUT = 2048
HEAD = 2048
EMBED = 128

TAU = 0.1
EPSILON = 1e-05
NORM_EPS = 1e-06
HIGHEST = lax.Precision.HIGHEST
BOTH = ("wide", "narrow")
BF16 = jnp.bfloat16
F32 = jnp.float32
DIMS = ("NHWC", "HWIO", "NHWC")


def device_count():
    return lax.axis_size("wide") * lax.axis_size("narrow")


def swap(values, mask):
    return lax.ppermute(values, BOTH, [(i, i ^ mask) for i in range(device_count())])


def bit_groups_of(count):
    groups = [[1]]
    bit = 2
    while bit < count:
        if 2 * bit < count:
            groups.append([bit, 2 * bit, 3 * bit])
        else:
            groups.append([bit])
        bit *= 4
    return groups


def bit_groups():
    return bit_groups_of(device_count())


def arrive(groups, values):
    values, arrivals = tied(values, [group.incoming for group in groups])
    for group, incoming in zip(groups, arrivals):
        group.incoming = incoming
    return values


def all_sum(values, groups=(), held=None, gate=None):
    stages = bit_groups()
    for stage, masks in enumerate(stages):
        if stage == 1 and gate is not None:
            _, gate = tied(values, gate)
        if stage == len(stages) - 1 and held is not None:
            values, held = step(groups, (values, held))
        others = [swap(values, mask) for mask in masks]
        values = values + others[0]
        if len(others) == 3:
            values = values + (others[1] + others[2])
    if held is None and gate is None:
        return values
    return (values, gate) if held is None else (values, held)


def gather_blocks(values):
    gathered = values[None]
    for masks in reversed(bit_groups()):
        gathered = jnp.concatenate([gathered] + [swap(gathered, mask) for mask in masks], axis=0)
    return gathered


def place_of(device, i, count):
    offset = jnp.bitwise_xor(device, i)
    place = jnp.int32(0)
    width = 0
    for masks in reversed(bit_groups_of(count)):
        bits = len(masks).bit_length()
        low = masks[0].bit_length() - 1
        place += ((offset >> low) & (2**bits - 1)) << width
        width += bits
    return place


def head_kernel(
    device,
    gathered,
    order,
    affine,
    flat,
    pooled_out,
    hidden_out,
    raw_cot_out,
    embed_cot,
    grads,
    losses,
    pooled_cot,
    rows_in,
    weights,
    embed_rows,
    w_embed,
    pooled,
    hidden,
    raw_cot,
    partners,
    terms,
    normed,
    slope,
    inv_std,
    embed,
    units,
    own_terms,
    own_wide,
    sems,
    out_sems,
):
    count, views_dev = gathered.shape[:2]
    total = count * views_dev
    tile = 256
    tiles = HEAD // tile

    def fetch(n):
        return pltpu.make_async_copy(
            flat.at[pl.ds(n * 4 * tile, 4 * tile), :], rows_in.at[n], sems.at[n]
        )

    def fetch_embed():
        return pltpu.make_async_copy(
            flat.at[pl.ds(4 * C_OUT, C_MID), :], embed_rows, sems.at[tiles]
        )

    def flush(source, target, n):
        return pltpu.make_async_copy(source, target, out_sems.at[n])

    for n in range(tiles):
        fetch(n).start()
    fetch_embed().start()

    for i in range(count):
        block = gathered[place_of(device[0], i, count)].astype(F32)
        pooled[i * views_dev : (i + 1) * views_dev, :] = block[:, :C_OUT]
        partners[i * views_dev : (i + 1) * views_dev, :] = block[:, C_OUT:]
    flush(pooled, pooled_out, 0).start()

    def halves(values):
        high = values.astype(BF16)
        return high, (values - high.astype(F32)).astype(BF16)

    def cut(n, carry):
        cols = pl.ds(pl.multiple_of(n * tile, tile), tile)
        terms[:, cols] = pooled[:, cols].astype(BF16)
        return carry

    lax.fori_loop(0, tiles, cut, 0)

    def unflatten_rows(n, carry):
        fetch(n).wait()
        for at in range(0, tile, 64):
            sorted_rows = jnp.dot(
                order[...], rows_in[n, 4 * at : 4 * at + 256, :], preferred_element_type=F32
            )
            for part in range(4):
                weights[
                    pl.ds(pl.multiple_of(n * tile + at, 64), 64), part * C_MID : (part + 1) * C_MID
                ] = sorted_rows[64 * part : 64 * part + 64, :].astype(BF16)
        return carry

    lax.fori_loop(0, tiles, unflatten_rows, 0)
    fetch_embed().wait()
    for part in range(4):
        embed_rows_wide = embed_rows[:, part * EMBED : (part + 1) * EMBED].astype(F32)
        own_wide[pl.ds(part, C_MID, stride=4), :] = embed_rows_wide
    w_embed[...] = own_wide[...].astype(BF16)
    embed[...] = jnp.zeros_like(embed)

    def forward(n, carry):
        cols = pl.ds(pl.multiple_of(n * tile, tile), tile)
        raw = jnp.dot(terms[...], weights[:, cols], preferred_element_type=F32)
        center = jnp.sum(raw, axis=0, keepdims=True) / total
        spread = jnp.sum(raw * raw, axis=0, keepdims=True) / total - center * center
        scale = lax.rsqrt(spread + EPSILON)
        unit = (raw - center) * scale
        shifted = unit * affine[0:1, cols] + affine[1:2, cols]
        logistic = jax.nn.sigmoid(shifted)
        value = shifted * logistic
        inv_std[:, cols] = scale
        normed[:, cols] = unit
        slope[:, cols] = logistic * (1.0 + shifted * (1.0 - logistic))
        hidden[:, cols] = value
        high, low = halves(value)
        embed[...] += jnp.dot(high, w_embed[cols, :], preferred_element_type=F32) + jnp.dot(
            low, w_embed[cols, :], preferred_element_type=F32
        )
        return carry

    lax.fori_loop(0, tiles, forward, 0)
    flush(hidden, hidden_out, 1).start()

    values = embed[...]
    length = lax.rsqrt(jnp.sum(values * values, axis=1, keepdims=True) + NORM_EPS)
    units[...] = jnp.zeros_like(units)
    units[:total, :] = (values * length).astype(BF16)
    every = units[...]
    size = every.shape[0]
    across = lax.broadcasted_iota(jnp.int32, (size, size), 0)
    along = lax.broadcasted_iota(jnp.int32, (size, size), 1)
    valid = (across != along) & (across < total) & (along < total)
    scores = (
        lax.dot_general(every, every, (((1,), (1,)), ((), ())), preferred_element_type=F32) / TAU
    )
    scores = jnp.where(valid, scores, -1e30)
    highest = jnp.max(scores, axis=1, keepdims=True)
    log_total = highest + jnp.log(jnp.sum(jnp.exp(scores - highest), axis=1, keepdims=True))
    chances = jnp.where(valid, jnp.exp(scores - log_total), 0.0)
    partner = (partners[:, 0:1] * 64.0 + partners[:, 1:2]).astype(jnp.int32)
    match = (along == partner) & valid
    loss = log_total - jnp.sum(jnp.where(match, scores, 0.0), axis=1, keepdims=True)
    losses[...] = jnp.broadcast_to(loss, losses.shape)
    near = chances - 2.0 * match.astype(F32)
    unit_cot = jnp.zeros((size, EMBED), F32)
    for part in halves(near):
        unit_cot += jnp.dot(part, every, preferred_element_type=F32)
    for part in halves(chances):
        unit_cot += lax.dot_general(
            part, every, (((0,), (0,)), ((), ())), preferred_element_type=F32
        )
    unit_cot = unit_cot[:total] * (1.0 / (total * TAU))
    along_cot = jnp.sum(values * unit_cot, axis=1, keepdims=True)
    cot = length * unit_cot - values * (length * length * length * along_cot)
    embed_cot[...] = cot
    cot_high, cot_low = halves(cot)
    rows = own_terms.shape[0] // 2
    chosen = lax.broadcasted_iota(jnp.int32, (rows, total), 1) == (
        device[0] * views_dev + lax.broadcasted_iota(jnp.int32, (rows, total), 0)
    )
    chosen = jnp.where(chosen, 1.0, 0.0).astype(BF16)

    def backward(n, carry):
        cols = pl.ds(pl.multiple_of(n * tile, tile), tile)
        pull = (((1,), (1,)), ((), ()))
        grad = lax.dot_general(
            cot_high, w_embed[cols, :], pull, preferred_element_type=F32
        ) + lax.dot_general(cot_low, w_embed[cols, :], pull, preferred_element_type=F32)
        grad = grad * slope[:, cols]
        unit = normed[:, cols]
        gain = jnp.sum(grad * unit, axis=0, keepdims=True)
        shift = jnp.sum(grad, axis=0, keepdims=True)
        grads[0:1, cols] = gain
        grads[1:2, cols] = shift
        raw = affine[0:1, cols] * inv_std[:, cols] * (grad - shift / total - unit * (gain / total))
        raw_cot[:, cols] = raw
        own = [
            jnp.dot(chosen, part, preferred_element_type=F32).astype(BF16) for part in halves(raw)
        ]
        own_terms[:, cols] = jnp.concatenate(own, axis=0)
        return carry

    lax.fori_loop(0, tiles, backward, 0)
    flush(raw_cot, raw_cot_out, 2).start()

    def pull_pooled(n, carry):
        at = pl.ds(pl.multiple_of(n * tile, tile), tile)
        product = lax.dot_general(
            own_terms[...],
            weights[at, :],
            (((1,), (1,)), ((), ())),
            preferred_element_type=F32,
        )
        pooled_cot[:, at] = product[:rows] + product[rows:]
        return carry

    lax.fori_loop(0, tiles, pull_pooled, 0)
    flush(pooled, pooled_out, 0).wait()
    flush(hidden, hidden_out, 1).wait()
    flush(raw_cot, raw_cot_out, 2).wait()


def head_pass(gathered, flat, affine):
    count, views_dev, width = gathered.shape
    total = count * views_dev
    size = -(-total // 256) * 256
    rows = 16
    tiles = HEAD // 256
    whole = pl.BlockSpec(memory_space=pltpu.VMEM)
    apart = pl.BlockSpec(memory_space=pl.ANY)
    shape = jax.ShapeDtypeStruct
    return pl.pallas_call(
        head_kernel,
        out_shape=[
            shape((total, C_OUT), F32),
            shape((total, HEAD), F32),
            shape((total, HEAD), F32),
            shape((total, EMBED), F32),
            shape((2, HEAD), F32),
            shape((size, EMBED), F32),
            shape((rows, C_OUT), F32),
        ],
        in_specs=[pl.BlockSpec(memory_space=pltpu.SMEM), whole, whole, whole, apart],
        out_specs=[apart] * 3 + [whole] * 4,
        scratch_shapes=[
            pltpu.VMEM((tiles, 1024, C_MID), BF16),
            pltpu.VMEM((C_OUT, HEAD), BF16),
            pltpu.VMEM((C_MID, C_MID), BF16),
            pltpu.VMEM((HEAD, EMBED), BF16),
            pltpu.VMEM((total, C_OUT), F32),
            pltpu.VMEM((total, HEAD), F32),
            pltpu.VMEM((total, HEAD), F32),
            pltpu.VMEM((size, width - C_OUT), F32),
            pltpu.VMEM((total, C_OUT), BF16),
            pltpu.VMEM((total, HEAD), F32),
            pltpu.VMEM((total, HEAD), F32),
            pltpu.VMEM((1, HEAD), F32),
            pltpu.VMEM((total, EMBED), F32),
            pltpu.VMEM((size, EMBED), BF16),
            pltpu.VMEM((2 * rows, HEAD), BF16),
            pltpu.VMEM((HEAD, EMBED), F32),
            pltpu.SemaphoreType.DMA((tiles + 1,)),
            pltpu.SemaphoreType.DMA((3,)),
        ],
        compiler_params=pltpu.CompilerParams(vmem_limit_bytes=52 << 20),
        cost_estimate=pl.CostEstimate(
            flops=4 * total * C_OUT * HEAD, bytes_accessed=20 << 20, transcendentals=3 * total * HEAD
        ),
    )(
        lax.axis_index(BOTH).reshape(1),
        gathered,
        jnp.asarray(row_order(), BF16),
        affine,
        flat,
    )


def copy_kernel(device, *refs):
    sources, target = refs[:-1], refs[-1]
    for way, source in enumerate(sources):
        target[way] = source[0]


def add_kernel(device, *refs):
    ways = len(refs) // 3
    for way in range(ways):
        first, second, target = refs[2 * way], refs[2 * way + 1], refs[2 * ways + way]
        target[...] = (first[...].astype(F32) + second[...].astype(F32)).astype(BF16)


def copy_blocks(source, count, place):
    block = (1, *source.shape[1:])
    shape = (count, *source.shape[1:])
    ways = min(count, 4)

    def read(way):
        return pl.BlockSpec(block, lambda i, device: (place(ways * i + way, device[0]), 0, 0))

    return pl.pallas_call(
        copy_kernel,
        out_shape=jax.ShapeDtypeStruct(shape, source.dtype),
        grid_spec=pltpu.PrefetchScalarGridSpec(
            num_scalar_prefetch=1,
            grid=(count // ways,),
            in_specs=[read(way) for way in range(ways)],
            out_specs=pl.BlockSpec((ways, *source.shape[1:]), lambda i, device: (i, 0, 0)),
        ),
        compiler_params=pltpu.CompilerParams(vmem_limit_bytes=24 << 20),
        cost_estimate=pl.CostEstimate(
            flops=0, bytes_accessed=4 * np.prod(shape).item(), transcendentals=0
        ),
    )(lax.axis_index(BOTH).reshape(1), *[source] * ways)


def add_blocks(source, incoming, count, places):
    ways = len(places)
    block = (1, *source.shape[1:])

    def read(place):
        return pl.BlockSpec(block, lambda i, device: (place(i, device[0]), 0, 0))

    shape = jax.ShapeDtypeStruct((count, *source.shape[1:]), BF16)
    size = np.prod(shape.shape).item()
    return pl.pallas_call(
        add_kernel,
        out_shape=[shape] * ways,
        grid_spec=pltpu.PrefetchScalarGridSpec(
            num_scalar_prefetch=1,
            grid=(count,),
            in_specs=[read(place) for pair in places for place in pair],
            out_specs=[pl.BlockSpec(block, lambda i, device: (i, 0, 0))] * ways,
        ),
        compiler_params=pltpu.CompilerParams(vmem_limit_bytes=24 << 20),
        cost_estimate=pl.CostEstimate(
            flops=size * ways, bytes_accessed=6 * size * ways, transcendentals=0
        ),
    )(lax.axis_index(BOTH).reshape(1), *([source, incoming] * ways))


class ScatterSum:
    def __init__(self, data, base, size):
        self.count = device_count()
        self.base = base
        self.size = size
        self.width = self.size
        self.source = data
        self.incoming = None
        self.folded = False
        self.live = [True] * self.count
        self.stage = 0
        self.stages = self.count.bit_length() - 1
        order = list(range(self.stages))
        if self.size > 8:
            other = [0, 2, 1] + order[3:]
        elif self.size == 8:
            other = [0, 2, 1] + order[4:] + [3]
        else:
            other = [0, 1] + order[3:] + [2]
        self.orders = [order, other]

    def bit(self, device):
        return self.orders[device & 1][self.stage]

    def halves(self, other):
        bits = [order[self.stage] for order in self.orders]
        ranks = [sorted(order[self.stage :]).index(order[self.stage]) for order in self.orders]

        def place(i, device):
            core = device & 1
            bit = bits[0] + core * (bits[1] - bits[0])
            at = ranks[0] + core * (ranks[1] - ranks[0])
            value = ((device >> bit) & 1) ^ int(other)
            return ((i >> at) << (at + 1)) | (value << at) | (i & ((1 << at) - 1))

        return place

    def within(self, place):
        if not self.folded:
            return place
        return lambda i, device: self.base + 2 * place(i, device) + (device & 1)

    def prepare(self):
        self.split = self.width > 1
        if self.split:
            self.width //= 2
            keep, send = self.halves(False), self.halves(True)
            if self.incoming is None:
                self.folded = True
                return copy_blocks(
                    self.source, self.width, lambda i, device: self.base + send(i, device)
                )
            self.source, outgoing = add_blocks(
                self.source,
                self.incoming,
                self.width,
                [(self.within(keep), keep), (self.within(send), send)],
            )
            self.folded = False
            return outgoing

        self.source = (self.source.astype(F32) + self.incoming.astype(F32)).astype(BF16)
        return self.source

    def send(self, outgoing):
        pairs = []
        for device in range(self.count):
            bit = 1 << self.bit(device)
            if self.split:
                pairs.append((device, device ^ bit))
            elif self.live[device] and (device ^ self.base) & bit:
                pairs.append((device, device ^ bit))
                self.live[device] = False
        self.incoming = lax.ppermute(outgoing, BOTH, pairs)
        self.stage += 1

    def done(self):
        return self.stage == self.stages

    def result(self):
        return self.source[0].astype(F32) + self.incoming[0].astype(F32)


def step(groups, held):
    groups = [group for group in groups if not group.done()]
    outgoing = [group.prepare() for group in groups]
    held, outgoing = lax.optimization_barrier((held, outgoing))
    for group, array in zip(groups, outgoing):
        group.send(array)
    return held


def row_order():
    order = np.zeros((256, 256), np.float32)
    for row in range(256):
        order[row, 4 * (row % 64) + row // 64] = 1.0
    return order


def unflatten_kernel(order, flat, target, rows_in, sems, *, first):
    tiles, rows = rows_in.shape[:2]

    def fetch(n):
        return pltpu.make_async_copy(
            flat.at[pl.ds(pl.multiple_of(first + n * rows, 256), rows), :], rows_in.at[n], sems.at[n]
        )

    for n in range(tiles):
        fetch(n).start()

    def sort_rows(n, carry):
        fetch(n).wait()
        for at in range(0, rows // 4, 64):
            sorted_rows = jnp.dot(
                order[...], rows_in[n, 4 * at : 4 * at + 256, :], preferred_element_type=F32
            )
            for part in range(4):
                target[
                    pl.ds(pl.multiple_of(n * (rows // 4) + at, 64), 64),
                    part * C_MID : (part + 1) * C_MID,
                ] = sorted_rows[64 * part : 64 * part + 64, :].astype(BF16)
        return carry

    lax.fori_loop(0, tiles, sort_rows, 0)


def unflatten(flat, first, rows):
    tile = 128

    def kernel(*refs):
        unflatten_kernel(*refs, first=first)

    return pl.pallas_call(
        kernel,
        out_shape=jax.ShapeDtypeStruct((rows, 4 * C_MID), BF16),
        in_specs=[
            pl.BlockSpec(memory_space=pltpu.VMEM),
            pl.BlockSpec(memory_space=pltpu.HBM),
        ],
        out_specs=pl.BlockSpec(memory_space=pltpu.VMEM),
        scratch_shapes=[
            pltpu.VMEM((rows // tile, 4 * tile, C_MID), BF16),
            pltpu.SemaphoreType.DMA((rows // tile,)),
        ],
        compiler_params=pltpu.CompilerParams(vmem_limit_bytes=24 << 20),
        cost_estimate=pl.CostEstimate(
            flops=2048 * rows * C_MID, bytes_accessed=16 * rows * C_MID, transcendentals=0
        ),
    )(jnp.asarray(row_order(), BF16), flat)


def flat_grad_kernel(inputs, cotan, *refs):
    target, scratch = refs[-2:]
    rows = inputs.shape[1]
    grad = lax.dot_general(
        inputs[...], cotan[...], (((0,), (0,)), ((), ())), preferred_element_type=F32
    )
    for lane in range(4):
        for part in range(4):
            at = part * C_MID + lane * 128
            scratch[lane, pl.ds(part, rows, stride=4), :] = grad[:, at : at + 128]
        target[:, lane * 128 : (lane + 1) * 128] = scratch[lane].astype(BF16)


def row_grad_kernel(inputs, cotan, *refs):
    refs[-1][...] = lax.dot_general(
        inputs[...], cotan[...], (((0,), (0,)), ((), ())), preferred_element_type=F32
    ).astype(BF16)


def grad_into(total, first, inputs, cotan, into=None):
    count, depth = inputs.shape
    width = cotan.shape[1]
    parts = width // C_MID
    if parts == 4:
        kernel, tile = flat_grad_kernel, 128
        scratch = [pltpu.VMEM((4, 4 * tile, 128), F32)]
    else:
        kernel, tile = row_grad_kernel, 256
        scratch = []
    at = first // (parts * tile)
    given = [] if into is None else [into]
    return pl.pallas_call(
        kernel,
        out_shape=jax.ShapeDtypeStruct((total, C_MID), BF16),
        grid=(depth // tile,),
        in_specs=[
            pl.BlockSpec((count, tile), lambda i: (0, i)),
            pl.BlockSpec((count, width), lambda i: (0, 0)),
        ]
        + [pl.BlockSpec(memory_space=pl.ANY) for _ in given],
        out_specs=pl.BlockSpec((parts * tile, C_MID), lambda i: (at + i, 0)),
        scratch_shapes=scratch,
        input_output_aliases={2: 0} if given else {},
        compiler_params=pltpu.CompilerParams(vmem_limit_bytes=24 << 20),
        cost_estimate=pl.CostEstimate(
            flops=2 * count * depth * width,
            bytes_accessed=2 * count * (depth + width) + 2 * depth * width,
            transcendentals=0,
        ),
    )(inputs, cotan, *given)


def split_norms(norm_params):
    widths = [C_MID, C_MID, C_OUT, C_OUT, C_MID, C_MID, C_OUT, HEAD]
    pieces = []
    offset = 0
    for span_width in widths:
        pieces.append(norm_params[:, offset : offset + span_width])
        offset += span_width
    return pieces


def moments(values):
    rows = values.reshape(-1, values.shape[-1])
    return jnp.stack([jnp.sum(rows, axis=0), jnp.sum(rows * rows, axis=0)])


def stats_of(sums, total_rows):
    center = sums[0] / total_rows
    inv_std = lax.rsqrt(sums[1] / total_rows - center * center + EPSILON)
    return center, inv_std


def silu_slope(values):
    logistic = jax.nn.sigmoid(values)
    return logistic * (1.0 + values * (1.0 - logistic))


class Norm:
    def __init__(self, raw, sums, affine, total_rows):
        self.raw = raw
        self.affine = affine
        self.total_rows = total_rows
        self.center, self.inv_std = stats_of(sums, total_rows)

    def normed(self):
        return (self.raw - self.center) * self.inv_std

    def shifted(self):
        return self.normed() * self.affine[0] + self.affine[1]

    def partial_grads(self, cotan):
        rows = cotan.reshape(-1, cotan.shape[-1])
        normed = self.normed().reshape(-1, cotan.shape[-1])
        return jnp.stack([jnp.sum(rows * normed, axis=0), jnp.sum(rows, axis=0)])

    def pull(self, cotan, grads):
        return (
            self.affine[0]
            * self.inv_std
            * (cotan - grads[1] / self.total_rows - self.normed() * (grads[0] / self.total_rows))
        )


def times(values, kernel):
    return jnp.dot(values, kernel, preferred_element_type=F32)


def times_back(cotan, kernel):
    return lax.dot_general(
        cotan, kernel, (((cotan.ndim - 1,), (1,)), ((), ())), preferred_element_type=F32
    )


def kernel_grad(inputs, cotan):
    return lax.dot_general(
        inputs.reshape(-1, inputs.shape[-1]),
        cotan.reshape(-1, cotan.shape[-1]),
        (((0,), (0,)), ((), ())),
        preferred_element_type=F32,
    )


def conv(values, kernel, stride):
    taps = kernel.reshape(3, 3, C_MID, C_MID)
    return lax.conv_general_dilated(
        values,
        taps,
        (stride, stride),
        ((1, 1), (1, 1)),
        dimension_numbers=DIMS,
        preferred_element_type=F32,
    )


def conv_back(cotan, kernel, stride):
    taps = kernel.reshape(3, 3, C_MID, C_MID)[::-1, ::-1].transpose(0, 1, 3, 2)
    after = stride
    return lax.conv_general_dilated(
        cotan,
        taps,
        (1, 1),
        ((1, after), (1, after)),
        lhs_dilation=(stride, stride),
        dimension_numbers=DIMS,
        preferred_element_type=F32,
    )


def conv_kernel_grad(values, cotan, stride):
    after = 2 - stride
    grad = lax.conv_general_dilated(
        values,
        cotan,
        (1, 1),
        ((1, after), (1, after)),
        rhs_dilation=(stride, stride),
        dimension_numbers=("CHWN", "IHWO", "HWNC"),
        preferred_element_type=F32,
    )
    return grad.reshape(9 * C_MID, C_MID)


def exact_times(values, kernel, contract):
    high = lax.reduce_precision(values, 8, 7)
    low = values - high
    count = values.shape[0]
    terms = jnp.concatenate([high, low], axis=0).astype(BF16)
    product = lax.dot_general(
        terms, kernel, (((1,), (contract,)), ((), ())), preferred_element_type=F32
    )
    return product[:count] + product[count:]


def pad_side(values, size):
    return lax.pad(
        values,
        jnp.zeros((), values.dtype),
        ((0, 0, 0), (0, 0, 0), (0, size - values.shape[2], 0), (0, 0, 0)),
    )


def even_cells_kernel(source, target, scratch):
    side = source.shape[1]
    scratch[...] = jnp.zeros_like(scratch)
    for lane in range(C_IN // 128):
        for row in range(0, side, 2):
            scratch[lane, 8 * row : 8 * row + side, :] = source[
                0, row, :, lane * 128 : (lane + 1) * 128
            ].astype(F32)
            target[0, row // 2, :, lane * 128 : (lane + 1) * 128] = scratch[
                lane, pl.ds(8 * row, 8, stride=2), :
            ].astype(BF16)


def even_cells(views):
    count, side = views.shape[:2]
    padded = pl.pallas_call(
        even_cells_kernel,
        out_shape=jax.ShapeDtypeStruct((count, side // 2, 8, C_IN), BF16),
        grid=(count,),
        in_specs=[pl.BlockSpec((1, side, side, C_IN), lambda i: (i, 0, 0, 0))],
        out_specs=pl.BlockSpec((1, side // 2, 8, C_IN), lambda i: (i, 0, 0, 0)),
        scratch_shapes=[pltpu.VMEM((C_IN // 128, side * 8, 128), F32)],
        compiler_params=pltpu.CompilerParams(vmem_limit_bytes=24 << 20),
        cost_estimate=pl.CostEstimate(
            flops=0, bytes_accessed=3 * count * side * side * C_IN, transcendentals=0
        ),
    )(views)
    return padded


def input_grad_kernel(cotan, kernel, strided, target, spread):
    side = target.shape[1]
    grad = lax.dot_general(
        cotan[0].reshape(-1, C_MID), kernel[...], (((1,), (1,)), ((), ())), preferred_element_type=F32
    )
    spread[...] = jnp.zeros_like(spread)
    for lane in range(C_IN // 128):
        for row in range(strided.shape[1]):
            spread[lane, pl.ds(32 * row, 8, stride=2), :] = strided[
                0, row, :, lane * 128 : (lane + 1) * 128
            ]
    for lane in range(C_IN // 128):
        total = grad[:, lane * 128 : (lane + 1) * 128] + spread[lane]
        target[0, :, :, lane * 128 : (lane + 1) * 128] = total.reshape(side, 16, 128)[:, :side, :]


def input_grad(cotan, kernel, strided):
    count, side = cotan.shape[:2]
    return pl.pallas_call(
        input_grad_kernel,
        out_shape=jax.ShapeDtypeStruct((count, side, side, C_IN), F32),
        grid=(count,),
        in_specs=[
            pl.BlockSpec((1, side, 16, C_MID), lambda i: (i, 0, 0, 0)),
            pl.BlockSpec((C_IN, C_MID), lambda i: (0, 0)),
            pl.BlockSpec((1, side // 2, 8, C_IN), lambda i: (i, 0, 0, 0)),
        ],
        out_specs=pl.BlockSpec((1, side, side, C_IN), lambda i: (i, 0, 0, 0)),
        scratch_shapes=[pltpu.VMEM((C_IN // 128, side * 16, 128), F32)],
        compiler_params=pltpu.CompilerParams(vmem_limit_bytes=24 << 20),
        cost_estimate=pl.CostEstimate(
            flops=2 * count * side * 16 * C_IN * C_MID,
            bytes_accessed=count * side * 16 * (2 * C_MID + 5 * C_IN),
            transcendentals=0,
        ),
    )(cotan, kernel, strided)


def silu_moments(mean, spread):
    nodes, weights = np.polynomial.hermite_e.hermegauss(5)
    weights = weights / weights.sum()
    values = [jax.nn.silu(mean + float(node) * jnp.sqrt(spread)) for node in nodes]
    first = sum(float(weight) * value for weight, value in zip(weights, values))
    second = sum(float(weight) * value * value for weight, value in zip(weights, values))
    return first, jnp.maximum(second - first * first, 0.0)


def pooled_center(main, short, last):
    joined, spread = silu_moments(main[1] + short[1], main[0] * main[0] + short[0] * short[0])
    return silu_moments(last[1] + joined, last[0] * last[0] + spread)[0]


def unit_norm(embed):
    return embed * lax.rsqrt(jnp.sum(embed * embed, axis=1, keepdims=True) + NORM_EPS)


def contrast(unit, partner, total_views):
    ids = jnp.arange(total_views, dtype=jnp.int32)
    scores = (
        lax.dot_general(unit, unit, (((1,), (1,)), ((), ())), preferred_element_type=F32) / TAU
    )
    scores = jnp.where(ids[None, :] == ids[:, None], -1e30, scores)
    highest = jnp.max(scores, axis=1)
    log_total = highest + jnp.log(jnp.sum(jnp.exp(scores - highest[:, None]), axis=1))
    match = ids[None, :] == partner[:, None]
    loss = log_total - jnp.sum(jnp.where(match, scores, 0.0), axis=1)
    weights = (
        jnp.exp(scores - log_total[:, None])
        + jnp.exp(scores - log_total[None, :])
        - 2.0 * match.astype(F32)
    ) * (1.0 / (total_views * TAU))
    unit_cot = jnp.dot(weights, unit.astype(F32), preferred_element_type=F32, precision=HIGHEST)
    return loss, unit_cot


def head_kernel_grads(pooled, raw_cot, hidden, embed_cot, block):
    first = lax.axis_index(BOTH) * block
    split = C_OUT * HEAD
    rows = -(-block // HEAD)
    if block % HEAD:
        rows += 1
    row_at = first // HEAD
    padded = jnp.pad(pooled, ((0, 0), (0, rows)))
    left = lax.dynamic_slice_in_dim(padded, jnp.minimum(row_at, C_OUT), rows, axis=1)
    hidden_part = lax.dot_general(
        left, raw_cot, (((0,), (0,)), ((), ())), preferred_element_type=F32, precision=HIGHEST
    ).reshape(-1)
    if block % HEAD:
        hidden_part = lax.dynamic_slice_in_dim(hidden_part, first - row_at * HEAD, block)
    embed_rows = block // EMBED
    padded = jnp.pad(hidden, ((0, 0), (embed_rows, embed_rows)))
    at = jnp.clip((first - split) // EMBED + embed_rows, 0, HEAD + embed_rows)
    left = lax.dynamic_slice_in_dim(padded, at, embed_rows, axis=1)
    embed_part = lax.dot_general(
        left, embed_cot, (((0,), (0,)), ((), ())), preferred_element_type=F32, precision=HIGHEST
    ).reshape(-1)
    place = first + jnp.arange(block, dtype=jnp.int32)
    return jnp.where(place < split, hidden_part, embed_part)


def placed(flat, at, piece):
    return lax.dynamic_update_slice(flat, piece.astype(BF16), (at, 0))


def cell_rows(values, size):
    return pad_side(values, size).reshape(-1, values.shape[-1])


def tied(*values):
    return lax.optimization_barrier(values)


def shards(views, partner, block1_params, block2_params, head_params, norm_params):
    views_dev = views.shape[0]
    count = device_count()
    total_views = views_dev * count
    device = lax.axis_index(BOTH)
    norms = split_norms(norm_params)

    def gather(flat):
        return lax.all_gather(flat.reshape(-1, C_MID), BOTH, axis=0, tiled=True)

    first = gather(block1_params)
    head = gather(head_params)
    second = gather(block2_params)
    strided = even_cells(views)
    full_views = pad_side(views, 16).reshape(-1, C_IN)
    first, strided, full_views = tied(first, strided, full_views)
    w_reduce = first[:1024]
    w_spatial = first[1024:5632]

    side = views.shape[1]
    wide_rows = total_views * side * side
    half = side // 2
    rows = total_views * half * half

    raw_one = times(views, w_reduce)
    norm_one = Norm(raw_one, all_sum(moments(raw_one)), norms[0], wide_rows)
    act_one = jax.nn.silu(norm_one.shifted()).astype(BF16)
    raw_two = conv(act_one, w_spatial, 2)
    w_expand = unflatten(first, 5632, C_MID)
    w_short = unflatten(first, 7680, C_IN)
    raw_short = times(strided, w_short)[:, :, :half]
    sums, w_expand, raw_short = tied(all_sum(moments(raw_two)), w_expand, raw_short)
    norm_two = Norm(raw_two, sums, norms[1], rows)
    act_two = jax.nn.silu(norm_two.shifted()).astype(BF16)
    raw_three = times(act_two, w_expand)
    sums = all_sum(jnp.concatenate([moments(raw_three), moments(raw_short)], axis=0))
    norm_three = Norm(raw_three, sums[:2], norms[2], rows)
    norm_short = Norm(raw_short, sums[2:], norms[3], rows)
    joined_one = norm_three.shifted() + norm_short.shifted()
    result_one = jax.nn.silu(joined_one).astype(BF16)

    w_narrow = second[:2048]
    w_middle = second[2048:6656]
    raw_five = times(result_one, w_narrow)
    norm_five = Norm(raw_five, all_sum(moments(raw_five)), norms[4], rows)
    act_three = jax.nn.silu(norm_five.shifted()).astype(BF16)
    raw_six = conv(act_three, w_middle, 1)
    w_widen = unflatten(second, 6656, C_MID)
    sums, w_widen = tied(all_sum(moments(raw_six)), w_widen)
    norm_six = Norm(raw_six, sums, norms[5], rows)
    act_four = jax.nn.silu(norm_six.shifted()).astype(BF16)
    raw_seven = times(act_four, w_widen)
    norm_seven = Norm(raw_seven, all_sum(moments(raw_seven)), norms[6], rows)
    joined_two = norm_seven.shifted() + result_one.astype(F32)
    pooled_own = jnp.mean(jax.nn.silu(joined_two), axis=(1, 2))

    center = pooled_center(norms[2], norms[3], norms[6])
    digits = jnp.stack([partner // 64, partner % 64], axis=1).astype(F32)
    gathered = gather_blocks(
        jnp.concatenate(
            [pooled_own - center, jnp.pad(digits, ((0, 0), (0, EMBED - 2)))], axis=1
        ).astype(BF16)
    )
    if total_views <= 256:
        pooled, hidden, raw_hidden_cot, embed_cot, grads_head, losses, pooled_cot = head_pass(
            gathered, head, norms[7]
        )
        losses = losses[:, 0]
        pooled_cot = pooled_cot[:views_dev]
    else:
        w_hidden = unflatten(head, 0, C_OUT)
        w_embed = head[4 * C_OUT :].reshape(HEAD, EMBED)
        order = jnp.stack([place_of(device, i, count) for i in range(count)])
        pooled = jnp.take(gathered, order, axis=0).reshape(total_views, -1).astype(F32)
        partners = (pooled[:, C_OUT] * 64.0 + pooled[:, C_OUT + 1]).astype(jnp.int32)
        pooled = pooled[:, :C_OUT]
        raw_hidden = exact_times(pooled, w_hidden, 0)
        norm_head = Norm(raw_hidden, moments(raw_hidden), norms[7], total_views)
        shifted_head = norm_head.shifted()
        hidden = jax.nn.silu(shifted_head)
        embed = exact_times(hidden, w_embed, 0)
        losses, unit_cot = contrast(unit_norm(embed).astype(BF16), partners, total_views)
        _, norm_pull = jax.vjp(unit_norm, embed)
        embed_cot = norm_pull(unit_cot)[0]
        hidden_cot = exact_times(embed_cot, w_embed, 1) * silu_slope(shifted_head)
        grads_head = norm_head.partial_grads(hidden_cot)
        raw_hidden_cot = norm_head.pull(hidden_cot, grads_head)
        own_cot = lax.dynamic_slice_in_dim(raw_hidden_cot, device * views_dev, views_dev, axis=0)
        pooled_cot = exact_times(own_cot, w_hidden, 1)

    joined_cot = (pooled_cot / (half * half))[:, None, None, :] * silu_slope(joined_two)
    loss = lax.dynamic_slice_in_dim(losses, device * views_dev, views_dev)
    grads_seven, loss = tied(all_sum(norm_seven.partial_grads(joined_cot)), loss)
    low_seven = norm_seven.pull(joined_cot, grads_seven).astype(BF16)
    act_four_cot = times_back(low_seven, w_widen) * silu_slope(norm_six.shifted())
    second_grad = grad_into(second.shape[0], 6656, cell_rows(act_four, 8), cell_rows(low_seven, 8))
    grads_six, second_grad = tied(all_sum(norm_six.partial_grads(act_four_cot)), second_grad)
    low_six = norm_six.pull(act_four_cot, grads_six).astype(BF16)
    act_three_cot = conv_back(low_six, w_middle, 1) * silu_slope(norm_five.shifted())
    second_grad = placed(second_grad, 2048, conv_kernel_grad(act_three, low_six, 1))
    grads_five, second_grad = tied(all_sum(norm_five.partial_grads(act_three_cot)), second_grad)
    low_five = norm_five.pull(act_three_cot, grads_five).astype(BF16)
    result_one_cot = joined_cot + times_back(low_five, w_narrow)

    joined_one_cot = result_one_cot * silu_slope(joined_one)
    grads_join = jnp.concatenate(
        [norm_three.partial_grads(joined_one_cot), norm_short.partial_grads(joined_one_cot)[:1]],
        axis=0,
    )
    second_grad = grad_into(
        second.shape[0], 0, cell_rows(result_one, 8), cell_rows(low_five, 8), second_grad
    )
    sum_second = ScatterSum(
        second_grad.reshape(count, second.shape[0] // count, C_MID), 0, count
    )
    grads_join, second_grad = all_sum(grads_join, [sum_second], second_grad)
    grads_three = grads_join[:2]
    grads_short = jnp.stack([grads_join[2], grads_join[1]])
    low_three = norm_three.pull(joined_one_cot, grads_three).astype(BF16)
    low_short = norm_short.pull(joined_one_cot, grads_short).astype(BF16)
    act_two_cot = times_back(low_three, w_expand) * silu_slope(norm_two.shifted())
    low_short = pad_side(low_short, 8)
    first_grad = grad_into(first.shape[0], 5632, cell_rows(act_two, 8), cell_rows(low_three, 8))
    first_grad = grad_into(
        first.shape[0],
        7680,
        strided.reshape(-1, C_IN),
        low_short.reshape(-1, C_OUT),
        first_grad,
    )
    grads_two = step([sum_second], norm_two.partial_grads(act_two_cot))
    grads_two, (head_rows, low_short) = all_sum(
        grads_two, gate=((pooled, raw_hidden_cot, hidden, embed_cot), low_short)
    )
    head_out = head_kernel_grads(*head_rows, head_params.shape[0])
    strided_cot = times_back(low_short, w_short)
    first_shape = (count, first.shape[0] // count, C_MID)
    first_blocks = first_grad.reshape(first_shape)
    part = count // 4
    late = ScatterSum(first_blocks, 2 * part, 2 * part)
    grads_two, first_grad, head_out, strided_cot = step(
        [sum_second, late], (grads_two, first_grad, head_out, strided_cot)
    )
    low_two = norm_two.pull(act_two_cot, grads_two).astype(BF16)
    act_one_cot = conv_back(low_two, w_spatial, 2)
    act_one_cot, first_grad = step([late], (act_one_cot, first_grad))
    act_one_cot = act_one_cot * silu_slope(norm_one.shifted())
    grads_one = norm_one.partial_grads(act_one_cot)
    grad_spatial = conv_kernel_grad(act_one, low_two, 2).astype(BF16)
    early_rows = part * first_shape[1]
    first_grad = placed(first_grad, early_rows, grad_spatial[early_rows - 1024 :])
    last_grad = jnp.pad(grad_spatial[: early_rows - 1024], ((1024, 0), (0, 0)))
    early = ScatterSum(first_grad.reshape(first_shape), part, part)
    grads_one, (first_grad, last_grad) = all_sum(grads_one, [early], (first_grad, last_grad))
    grads_one, first_grad, last_grad = step(
        [early, late], (grads_one, first_grad, last_grad)
    )
    low_one = pad_side(norm_one.pull(act_one_cot, grads_one).astype(BF16), 16)
    last_grad = grad_into(early_rows, 0, full_views, low_one.reshape(-1, C_MID), last_grad)
    last_grad = arrive([late], last_grad)
    last = ScatterSum(last_grad.reshape(part, *first_shape[1:]), 0, part)
    low_one = step([last, sum_second], low_one)
    views_cot = input_grad(low_one, w_reduce, strided_cot)
    groups = [early, last, late, sum_second]
    while any(not group.done() for group in groups):
        for group in groups:
            if not group.done():
                group.send(group.prepare())

    second_out = sum_second.result().reshape(-1)
    first_out = last.result()
    for group in [early, late]:
        first_out = jnp.where(device < group.base, first_out, group.result())
    first_out = first_out.reshape(-1)
    norm_grad = jnp.concatenate(
        [
            grads_one,
            grads_two,
            grads_three,
            grads_short,
            grads_five,
            grads_six,
            grads_seven,
            grads_head,
        ],
        axis=1,
    )
    return (loss, views_cot, first_out, second_out, head_out, norm_grad)


def solution(mesh):
    return jax.shard_map(
        shards,
        mesh=mesh,
        in_specs=(
            P(BOTH, None, None, None),
            P(BOTH),
            P(BOTH),
            P(BOTH),
            P(BOTH),
            P(),
        ),
        out_specs=(
            P(BOTH),
            P(BOTH, None, None, None),
            P(BOTH),
            P(BOTH),
            P(BOTH),
            P(),
        ),
        check_vma=False,
    )
```
